128 devices in a mesh: rep: 16 (over x, z), tp: 8 (over y, core).
Axes of the slice: x: 4, y: 4, z: 4, core: 2. Of those that a mesh axis runs over, the one named last changes fastest.
Arguments:
- hidden: bfloat16 [16384, 8192], P('rep', 'tp'), may hold values from -6 to 6
- w_query: bfloat16 [8192, 4096], P(None, 'tp'), may hold values from -1 to 1
- w_keyval: bfloat16 [8192, 2048], P(None, 'tp'), may hold values from -1 to 1
- kv_pool: bfloat16 [2048, 128, 2048], P('rep', None, 'tp'), may hold values from -240 to 240
- prefix_len: int32 [128], replicated, may hold values from 1 to 2048, 65536 in all
- owner: int32 [128], replicated, may hold values from 0 to 15, as said below
- block_table: int32 [128, 16], replicated, may hold values from 0 to 127, as said below
Outputs:
- attended: bfloat16 [16384, 4096], P('rep', 'tp')
- new_cache: bfloat16 [128, 128, 2048], P('rep', None, 'tp')
The draws below stay inside these ranges and needn't reach their ends.
Inputs may be any that keep to these rules, and one draw needn't show every extreme that they name: `owner`: the 8 spans of one replica (entries r * 8 onward) have distinct owners, and every replica owns exactly one span c with c % 8 == k for each k. `block_table`: each row lists distinct pages of the owner's pool; the rows of the spans one replica owns use every page of its pool exactly once.
All inputs are finite; a program needn't handle non-finite values.
Results may differ from the reference program's by a relative error of at most 0.011.
Values may be sent and summed in bfloat16 or wider, within the bound.
A program may use at most 192 MiB of HBM per device.

```python
import math
import jax
import jax.numpy as jnp
import numpy as np
from jax import lax

D = 8192
KV_HEADS = 8
HEAD_DIM = 128
HEADS = 32
SPAN_DEV = 8
SPAN_LEN = 128
PREFIX_MAX = 2048
PAGE = 128
PAGES_SEQ = 16
POOL_DEV = 128
POOL_ALL = 2048
SPANS = 128
TOKENS = 16384
N_REP = 16


def owner_table(key):
    replicas = SPANS // SPAN_DEV
    key_order, key_offset = jax.random.split(key)
    shuffle = jax.random.permutation(key_order, replicas)
    offsets = jax.random.permutation(key_offset, replicas)[:SPAN_DEV]
    source = jnp.arange(SPANS, dtype=jnp.int32)
    return shuffle[(source // SPAN_DEV + offsets[source % SPAN_DEV]) % replicas].astype(jnp.int32)


def draw_owner(key, part):
    return owner_table(key)


def draw_block_table(key, part):
    owners = owner_table(key)
    key = jax.random.fold_in(key, 2)
    replicas = SPANS // SPAN_DEV
    orders = jax.vmap(lambda subkey: jax.random.permutation(subkey, POOL_DEV))(jax.random.split(key, replicas))
    span_ids = jnp.arange(SPANS, dtype=jnp.int32)
    slot_index = (span_ids % SPAN_DEV)[:, None] * PAGES_SEQ + jnp.arange(PAGES_SEQ, dtype=jnp.int32)[None, :]
    return orders[owners[:, None], slot_index].astype(jnp.int32)


def draw_kv_pool(key, part):
    key = jax.random.fold_in(key, 1)
    shape = (POOL_ALL, PAGE, KV_HEADS * 2 * HEAD_DIM)
    values = jnp.clip(jax.random.normal(key, shape, jnp.float32), -6.0, 6.0)
    return values.astype(jnp.bfloat16)


def draw_hidden(key, part):
    folded = jax.random.fold_in(key, 4)
    shape = (TOKENS, D)
    values = jnp.clip(jax.random.normal(folded, shape, jnp.float32), -6.0, 6.0)
    return values.astype(jnp.bfloat16)


def draw_w_query(key, part):
    folded = jax.random.fold_in(key, 5)
    shape = (D, HEADS * HEAD_DIM)
    values = jnp.clip(jax.random.normal(folded, shape, jnp.float32), -6.0, 6.0) * D ** (-0.5)
    return values.astype(jnp.bfloat16)


def draw_w_keyval(key, part):
    folded = jax.random.fold_in(key, 6)
    shape = (D, KV_HEADS * 2 * HEAD_DIM)
    values = jnp.clip(jax.random.normal(folded, shape, jnp.float32), -6.0, 6.0) * D ** (-0.5)
    return values.astype(jnp.bfloat16)


def split_up(count, total, most, lean):
    portions = [(1 << 20) // math.isqrt(rank ** lean) + 1 for rank in range(2, count + 1)]
    rest, holding = total - most - (count - 1), [1] * (count - 1)
    while rest > 0:
        movable = [i for i in range(count - 1) if holding[i] < most]
        pool, remaining = sum([portions[i] for i in movable]), rest
        for i in movable:
            extra = min(most - holding[i], max(1, remaining * portions[i] // pool), rest)
            holding[i] = holding[i] + extra
            rest = rest - extra
    return np.array([most] + holding)


def uneven(stream_key, amount, total, reach, slope):
    if amount == 2:
        one = jax.random.randint(stream_key, (), max(1, total - reach), min(reach, total - 1) + 1)
        return jnp.stack([one, total - one])
    lengths = jnp.asarray(split_up(amount, total, reach, slope), jnp.int32)
    pairs = (amount - 1) // 2
    donor, receiver = lengths[1:1 + 2 * pairs:2], lengths[2:2 + 2 * pairs:2]
    room = jnp.minimum(donor - 1, reach - receiver)
    moved = jax.random.randint(jax.random.fold_in(stream_key, 1), (pairs,), 0, 1 << 20) % (room + 1)
    lengths = lengths.at[1:1 + 2 * pairs:2].set(donor - moved).at[2:2 + 2 * pairs:2].set(receiver + moved)
    return lengths[jax.random.permutation(jax.random.fold_in(stream_key, 2), amount)]


def setup_inputs(seed: int = 0) -> dict:
    key_of = jax.random.split(jax.random.key(seed), 8)
    hidden = draw_hidden(jax.random.fold_in(key_of[7], 71), 0)
    w_query = draw_w_query(jax.random.fold_in(key_of[7], 71), 0)
    w_keyval = draw_w_keyval(jax.random.fold_in(key_of[7], 71), 0)
    kv_pool = draw_kv_pool(jax.random.fold_in(key_of[7], 71), 0)
    prefix_len = uneven(key_of[4], SPANS, SPANS * PREFIX_MAX // 4, PREFIX_MAX, 2).astype(jnp.int32)
    owner = draw_owner(jax.random.fold_in(key_of[7], 71), 0)
    block_table = draw_block_table(jax.random.fold_in(key_of[7], 71), 0)
    return dict(hidden=hidden, w_query=w_query, w_keyval=w_keyval, kv_pool=kv_pool, prefix_len=prefix_len, owner=owner, block_table=block_table)


ROPE_BASE = 500000.0

def rotate(values, positions):
    half_dim = values.shape[-1] // 2
    frequency = ROPE_BASE ** (-jnp.arange(half_dim, dtype=jnp.float32) * 2.0 / values.shape[-1])
    angles = positions.astype(jnp.float32)[..., None] * frequency
    cosine = jnp.cos(angles)
    sine_part = jnp.sin(angles)
    front = values[..., :half_dim]
    back_half = values[..., half_dim:]
    return jnp.concatenate([front * cosine - back_half * sine_part, back_half * cosine + front * sine_part], axis=-1)

def reference(hidden, w_query, w_keyval, kv_pool, prefix_len, owner, block_table):
    group = HEADS // KV_HEADS
    scale_factor = 1.0 / math.sqrt(HEAD_DIM)
    query = jnp.dot(hidden, w_query, preferred_element_type=jnp.float32)
    keyval = jnp.dot(hidden, w_keyval, preferred_element_type=jnp.float32)
    offsets = jnp.arange(SPAN_LEN, dtype=jnp.int32)
    positions = prefix_len[:, None] + offsets[None, :]
    query = query.reshape(SPANS, SPAN_LEN, HEADS, HEAD_DIM)
    q_rot = rotate(query, positions[:, :, None]).astype(jnp.bfloat16)
    q_rot = q_rot.reshape(SPANS, SPAN_LEN, KV_HEADS, group, HEAD_DIM)
    keyval = keyval.reshape(SPANS, SPAN_LEN, KV_HEADS, 2 * HEAD_DIM)
    fresh = jnp.concatenate([rotate(keyval[..., :HEAD_DIM], positions[:, :, None]), keyval[..., HEAD_DIM:]], axis=-1).astype(jnp.bfloat16)
    pages = kv_pool.reshape(N_REP, POOL_DEV, PAGE, KV_HEADS, 2 * HEAD_DIM)
    span_index = jnp.arange(PREFIX_MAX, dtype=jnp.int32)
    causal = offsets[:, None] >= offsets[None, :]

    def one_span(span):
        prefix = pages[owner[span]][block_table[span]].reshape(PREFIX_MAX, KV_HEADS, 2 * HEAD_DIM)
        keys_all = jnp.concatenate([prefix, fresh[span]], axis=0).astype(jnp.float32)
        visible = jnp.concatenate([jnp.broadcast_to(span_index[None, :] < prefix_len[span], (SPAN_LEN, PREFIX_MAX)), causal], axis=1)
        scores = jnp.einsum('ckgd,skd->ckgs', q_rot[span].astype(jnp.float32), keys_all[..., :HEAD_DIM], precision=lax.Precision.HIGHEST) * scale_factor
        scores = jnp.where(visible[:, None, None, :], scores, -jnp.inf)
        highest = lax.optimization_barrier(jnp.max(scores, axis=-1))
        weights = jnp.exp(scores - highest[..., None])
        totals = lax.optimization_barrier(jnp.sum(weights, axis=-1))
        rounded = lax.optimization_barrier(weights.astype(jnp.bfloat16)).astype(jnp.float32)
        summed = jnp.einsum('ckgs,skd->ckgd', rounded, keys_all[..., HEAD_DIM:], precision=lax.Precision.HIGHEST)
        return (summed / totals[..., None]).reshape(SPAN_LEN, HEADS * HEAD_DIM).astype(jnp.bfloat16)
    attended = lax.map(one_span, jnp.arange(SPANS, dtype=jnp.int32))
    targets = owner * SPAN_DEV + jnp.arange(SPANS, dtype=jnp.int32) % SPAN_DEV
    new_cache = jnp.zeros((SPANS, SPAN_LEN, KV_HEADS * 2 * HEAD_DIM), jnp.bfloat16)
    new_cache = new_cache.at[targets].set(fresh.reshape(SPANS, SPAN_LEN, KV_HEADS * 2 * HEAD_DIM))
    return (attended.reshape(TOKENS, HEADS * HEAD_DIM), new_cache)
```

```python
import math

import jax
import jax.numpy as jnp
import numpy as np
from jax import lax
from jax.experimental import pallas as pl
from jax.experimental.pallas import tpu as pltpu
from jax.sharding import PartitionSpec as P

HEAD_DIM = 128
SPAN_LEN = 128
ROPE_BASE = 500000.0
MESH = pl.DeviceIdType.MESH
BF = jnp.bfloat16
F32 = jnp.float32

REPS = 16
STEPS = 8
PAGES = 16
GROUP = 4
ROWS = GROUP * SPAN_LEN
MSG = ROWS + 2 * SPAN_LEN
PIECE = MSG // REPS
BACK = ROWS // REPS
KEYS = PAGES * 128 + SPAN_LEN
CHUNK = 1024
NEAR = 6 * CHUNK
SCALE = 1.0 / math.sqrt(HEAD_DIM)
LOG2E = math.log2(math.e)

T_LEN = SPAN_LEN * PAGES
T_OWN = T_LEN + 128
T_INV = T_OWN + 128


def kernel(
    table, hid, wq_h, wkv_h, pool_h, trig, out, cache,
    gath, wq, wkv, pool, accq, acck, msg, r1, st2, r2, om, r3, st4, r4, scores, work1, work3,
    local_sem, y_send, y_recv, x_send, x_recv,
):
    me = lax.axis_index("rep")
    tp = lax.axis_index("tp")
    y, c = tp // 2, lax.rem(tp, 2)
    up = (me, lax.rem(y + 1, 4) * 2 + c)
    down = (me, lax.rem(y + 3, 4) * 2 + c)
    sib = (me, y * 2 + 1 - c)

    loads = []
    for slot, (rel, other) in enumerate(
        [(0, 0), (0, 1), (3, 0), (1, 0), (3, 1), (1, 1), (2, 0), (2, 1)]
    ):
        core = c if other == 0 else 1 - c
        rows = pl.ds(pl.multiple_of((lax.rem(y + rel, 4) * 2 + core) * CHUNK, CHUNK), CHUNK)
        place = pl.ds(slot * CHUNK, CHUNK)
        loads.append(pltpu.make_async_copy(wq_h.at[rows], wq.at[place], local_sem.at[2 * slot]))
        loads.append(
            pltpu.make_async_copy(wkv_h.at[rows], wkv.at[place], local_sem.at[2 * slot + 1])
        )
    for s in range(STEPS):
        loads.append(
            pltpu.make_async_copy(
                hid.at[pl.ds(s * SPAN_LEN, SPAN_LEN)],
                gath.at[s, :, pl.ds(0, CHUNK)],
                local_sem.at[16 + s],
            )
        )
    loads.append(pltpu.make_async_copy(pool_h, pool, local_sem.at[24]))
    for load in loads:
        load.start()

    barrier = pltpu.get_barrier_semaphore()
    for device in (up, down, sib):
        pl.semaphore_signal(barrier, inc=1, device_id=device, device_id_type=MESH)
    for d in range(1, REPS):
        pl.semaphore_signal(
            barrier, inc=1, device_id=(lax.rem(me + d, REPS), tp), device_id_type=MESH
        )
    pl.semaphore_wait(barrier, 3 + REPS - 1)

    def remote(src, dst, send, recv, device):
        return pltpu.make_async_remote_copy(
            src_ref=src, dst_ref=dst, send_sem=send, recv_sem=recv,
            device_id=device, device_id_type=MESH,
        )

    def part(s, slot, first=0, count=SPAN_LEN):
        return gath.at[s, pl.ds(first, count), pl.ds(slot * CHUNK, CHUNK)]

    half = SPAN_LEN // 2

    def y_copy(kind, s):
        own = hid.at[pl.ds(pl.multiple_of(s * SPAN_LEN, SPAN_LEN), SPAN_LEN)]
        sems = (y_send.at[kind, s], y_recv.at[kind, s])
        if kind == 0:
            return remote(own, part(s, 2), *sems, up)
        if kind == 1:
            return remote(own, part(s, 3), *sems, down)
        if kind == 2:
            return remote(own, part(s, 1), *sems, sib)
        if kind == 3:
            return remote(part(s, 2, 0, half), part(s, 6, 0, half), *sems, up)
        if kind == 4:
            return remote(part(s, 3, half, half), part(s, 6, half, half), *sems, down)
        if kind == 5:
            return remote(part(s, 2), part(s, 4), *sems, sib)
        if kind == 6:
            return remote(part(s, 3), part(s, 5), *sems, sib)
        return remote(part(s, 6), part(s, 7), *sems, sib)

    def near_send(s):
        for kind in (0, 1, 2):
            y_copy(kind, s).start()

    def exchange(phase, s, src, dst):
        def one(d, carry):
            target = lax.rem(me + d, REPS)
            remote(
                src.at[s, target], dst.at[s, me], x_send.at[phase, s], x_recv.at[phase, s],
                (target, tp),
            ).start()
            return carry

        lax.fori_loop(1, REPS, one, 0, unroll=True)
        dst[s, me] = src[s, me]

    def landed(phase, s, dst):
        ref = dst.at[s, pl.ds(0, REPS - 1)]
        pltpu.make_async_copy(ref, ref, x_recv.at[phase, s]).wait()

    def sent(phase, s, src):
        ref = src.at[s, pl.ds(0, REPS - 1)]
        pltpu.make_async_copy(ref, ref, x_send.at[phase, s]).wait()

    near_send(0)
    near_send(1)
    for load in loads:
        load.wait()

    lane = lax.broadcasted_iota(jnp.int32, (1, 128), 1)

    def project_near(s):
        slot = lax.rem(s, 2)
        x = gath[s, :, :NEAR]
        accq[slot] = jnp.dot(x, wq[:NEAR], preferred_element_type=F32)
        acck[slot] = jnp.dot(x, wkv[:NEAR], preferred_element_type=F32)

    def project_far(s):
        slot = lax.rem(s, 2)
        x = gath[s, :, NEAR:]
        query = accq[slot] + jnp.dot(x, wq[NEAR:], preferred_element_type=F32)
        keyval = acck[slot] + jnp.dot(x, wkv[NEAR:], preferred_element_type=F32)
        start = table[T_LEN + me * STEPS + s].astype(F32)
        angle = start * trig[2, :8]
        cos_p, sin_p = jnp.cos(angle)[:1], jnp.sin(angle)[:1]
        cos_t, sin_t = trig[0], trig[1]
        cosine = cos_p * cos_t - sin_p * sin_t
        sine = sin_p * cos_t + cos_p * sin_t
        sine = jnp.where(lane < HEAD_DIM // 2, -sine, sine)

        def rotate(v):
            return (v * cosine + pltpu.roll(v, HEAD_DIM // 2, 1) * sine).astype(BF)

        blocks = [rotate(query[:, h * 128 : (h + 1) * 128]) for h in range(GROUP)]
        blocks.append(rotate(keyval[:, :128]))
        blocks.append(keyval[:, 128:].astype(BF))
        msg[s] = jnp.concatenate(blocks, axis=0).reshape(REPS, PIECE, 128)

    def attend(s):
        row = table[T_INV + s * REPS + me] * STEPS + s
        length = table[T_LEN + row]
        whole = r2[s].reshape(MSG, 128)
        q = whole[:ROWS]
        fresh_k, fresh_v = whole[ROWS : ROWS + 128], whole[ROWS + 128 :]
        cache[s, :, :128] = fresh_k
        cache[s, :, 128:] = fresh_v
        nt = (((1,), (1,)), ((), ()))

        def page(j):
            return pool[table[row * PAGES + j]]

        t = lax.rem(lax.broadcasted_iota(jnp.int32, (ROWS, 128), 0), SPAN_LEN)
        t_key = lax.broadcasted_iota(jnp.int32, (ROWS, 128), 1)
        sc = lax.dot_general(q, fresh_k, nt, preferred_element_type=F32)
        sc = jnp.where(t_key <= t, sc, -jnp.inf)
        scores[:, PAGES * 128 :] = sc
        top = sc
        position = lax.broadcasted_iota(jnp.int32, (1, 256), 1)
        for j in range(0, PAGES, 2):
            keys = jnp.concatenate([page(j)[:, :128], page(j + 1)[:, :128]], axis=0)
            bias = jnp.where(position + j * 128 < length, 0.0, -jnp.inf)
            sc = lax.dot_general(q, keys, nt, preferred_element_type=F32) + bias
            scores[:, j * 128 : (j + 2) * 128] = sc
            top = jnp.maximum(top, jnp.maximum(sc[:, :128], sc[:, 128:]))
        factor = SCALE * LOG2E
        highest = jnp.max(top, axis=1, keepdims=True) * factor
        w = jnp.exp2(scores[:, PAGES * 128 :] * factor - highest)
        total = w
        summed = jnp.dot(w.astype(BF), fresh_v, preferred_element_type=F32)
        for j in range(0, PAGES, 2):
            values = jnp.concatenate([page(j)[:, 128:], page(j + 1)[:, 128:]], axis=0)
            w = jnp.exp2(scores[:, j * 128 : (j + 2) * 128] * factor - highest)
            total = total + (w[:, :128] + w[:, 128:])
            summed = summed + jnp.dot(w.astype(BF), values, preferred_element_type=F32)
        total = jnp.sum(total, axis=1, keepdims=True)
        om[s] = (summed / total).astype(BF).reshape(REPS, BACK, 128)

    def when(s):
        return pl.when((s >= 0) & (s < STEPS))

    def step(it, carry):
        @when(it + 2)
        def _():
            near_send(it + 2)

        @when(it)
        def _():
            y_copy(0, it).wait_recv()
            y_copy(3, it).start()
            y_copy(5, it).start()
            y_copy(1, it).wait_recv()
            y_copy(4, it).start()
            y_copy(6, it).start()

        @when(it - 1)
        def _():
            y_copy(3, it - 1).wait_recv()
            y_copy(4, it - 1).wait_recv()
            y_copy(7, it - 1).start()

        @when(it - 2)
        def _():
            s = it - 2
            landed(0, s, r1)
            work1[...] = r1[s]
            for o in range(REPS):
                st2[s, o] = work1[table[T_INV + s * REPS + o]]
            exchange(1, s, st2, r2)

        @when(it - 4)
        def _():
            s = it - 4
            landed(2, s, r3)
            work3[...] = r3[s]
            for r in range(REPS):
                st4[s, r] = work3[table[T_OWN + r * STEPS + s]]
            exchange(3, s, st4, r4)

        @when(it)
        def _():
            for kind in (2, 5, 6):
                y_copy(kind, it).wait_recv()
            project_near(it)

        @when(it - 1)
        def _():
            y_copy(7, it - 1).wait_recv()
            project_far(it - 1)
            exchange(0, it - 1, msg, r1)

        @when(it - 3)
        def _():
            landed(1, it - 3, r2)
            attend(it - 3)
            exchange(2, it - 3, om, r3)

        @when(it - 5)
        def _():
            s = it - 5
            landed(3, s, r4)
            rows = pl.ds(pl.multiple_of(s * SPAN_LEN, SPAN_LEN), SPAN_LEN)
            whole = r4[s].reshape(ROWS, 128)
            for h in range(GROUP):
                out[rows, h * 128 : (h + 1) * 128] = whole[h * 128 : (h + 1) * 128]

        return carry

    lax.fori_loop(0, STEPS + 5, step, 0)

    def drain(s, carry):
        for kind in range(8):
            y_copy(kind, s).wait_send()
        sent(0, s, msg)
        sent(1, s, st2)
        sent(2, s, om)
        sent(3, s, st4)
        return carry

    lax.fori_loop(0, STEPS, drain, 0)


def trig_tables():
    i = np.arange(64, dtype=np.float64)
    frequency = np.concatenate([ROPE_BASE ** (-2.0 * i / HEAD_DIM)] * 2)
    angle = np.arange(SPAN_LEN, dtype=np.float64)[:, None] * frequency[None, :]
    wide = np.broadcast_to(frequency[None, :], (SPAN_LEN, HEAD_DIM))
    return np.stack([np.cos(angle), np.sin(angle), wide]).astype(np.float32)


def body(hidden, w_query, w_keyval, kv_pool, prefix_len, owner, block_table):
    by_step = owner.reshape(REPS, STEPS).T
    ids = jnp.arange(REPS, dtype=jnp.int32)
    inverse = jnp.sum(
        jnp.where(by_step[:, None, :] == ids[None, :, None], ids[None, None, :], 0), axis=2
    )
    table = jnp.concatenate(
        [block_table.reshape(-1), prefix_len, owner, inverse.reshape(-1).astype(jnp.int32)]
    )
    v = pltpu.VMEM
    dma = pltpu.SemaphoreType.DMA
    any_spec = pl.BlockSpec(memory_space=pl.ANY)
    vmem = pl.BlockSpec(memory_space=pltpu.VMEM)
    return pl.pallas_call(
        kernel,
        out_shape=(
            jax.ShapeDtypeStruct((STEPS * SPAN_LEN, GROUP * 128), BF),
            jax.ShapeDtypeStruct((STEPS, SPAN_LEN, 256), BF),
        ),
        in_specs=[pl.BlockSpec(memory_space=pltpu.SMEM)] + [any_spec] * 4 + [vmem],
        out_specs=(vmem, vmem),
        scratch_shapes=[
            v((STEPS, SPAN_LEN, 8 * CHUNK), BF),
            v((8 * CHUNK, GROUP * 128), BF),
            v((8 * CHUNK, 256), BF),
            v((128, 128, 256), BF),
            v((2, SPAN_LEN, GROUP * 128), F32),
            v((2, SPAN_LEN, 256), F32),
            v((STEPS, REPS, PIECE, 128), BF),
            v((STEPS, REPS, PIECE, 128), BF),
            v((STEPS, REPS, PIECE, 128), BF),
            v((STEPS, REPS, PIECE, 128), BF),
            v((STEPS, REPS, BACK, 128), BF),
            v((STEPS, REPS, BACK, 128), BF),
            v((STEPS, REPS, BACK, 128), BF),
            v((STEPS, REPS, BACK, 128), BF),
            v((ROWS, KEYS), F32),
            v((REPS, PIECE, 128), BF),
            v((REPS, BACK, 128), BF),
            dma((25,)),
            dma((8, STEPS)),
            dma((8, STEPS)),
            dma((4, STEPS)),
            dma((4, STEPS)),
        ],
        compiler_params=pltpu.CompilerParams(
            collective_id=0, has_side_effects=True, vmem_limit_bytes=62 * 1024 * 1024
        ),
        cost_estimate=pl.CostEstimate(
            flops=18_000_000_000, bytes_accessed=24_000_000, transcendentals=9_000_000
        ),
    )(table, hidden, w_query, w_keyval, kv_pool, jnp.asarray(trig_tables()))


def solution(mesh):
    placed = (P("rep", "tp"), P(None, "tp"), P(None, "tp"), P("rep", None, "tp"), P(), P(), P())
    return jax.shard_map(
        body,
        mesh=mesh,
        in_specs=placed,
        out_specs=(P("rep", "tp"), P("rep", None, "tp")),
        check_vma=False,
    )
```

```python
import math

import jax
import jax.numpy as jnp
import numpy as np
from jax import lax
from jax.experimental import pallas as pl
from jax.experimental.pallas import tpu as pltpu
from jax.sharding import PartitionSpec as P

HEAD_DIM = 128
SPAN_LEN = 128
ROPE_BASE = 500000.0
MESH = pl.DeviceIdType.MESH
BF = jnp.bfloat16
F32 = jnp.float32

REPS = 16
STEPS = 8
PAGES = 16
GROUP = 4
ROWS = GROUP * SPAN_LEN
MSG = ROWS + 2 * SPAN_LEN
PIECE = MSG // REPS
BACK = ROWS // REPS
KEYS = PAGES * 128 + SPAN_LEN
CHUNK = 1024
NEAR = 6 * CHUNK
SCALE = 1.0 / math.sqrt(HEAD_DIM)
LOG2E = math.log2(math.e)

EARLY = 2
LATE = STEPS - EARLY
HALF = CHUNK // 2
BLOCK = 256
OFFSETS = [
    (2, 2), (2, 1), (1, 2), (2, 3), (3, 2), (1, 1), (3, 3), (1, 3), (3, 1),
    (0, 2), (2, 0), (0, 1), (1, 0), (0, 3), (3, 0),
]


def kernel(
    lens, owner, pages, hid, wq_h, wkv_h, pool_h, trig, out, cache,
    gath, wq, wkv, pool, accq, acck, hv, rh, sth, msg, r1, st2, r2, om, r3, st4, r4,
    scores, workh, work1, work3,
    local_sem, y_send, y_recv, x_send, x_recv,
):
    me = lax.axis_index("rep")
    tp = lax.axis_index("tp")
    y, c = tp // 2, lax.rem(tp, 2)
    up = (me, lax.rem(y + 1, 4) * 2 + c)
    down = (me, lax.rem(y + 3, 4) * 2 + c)
    sib = (me, y * 2 + 1 - c)
    peers = [
        lax.rem(me // 4 + dx, 4) * 4 + lax.rem(lax.rem(me, 4) + dz, 4) for dx, dz in OFFSETS
    ]

    loads = []

    def load(src, dst):
        loads.append(pltpu.make_async_copy(src, dst, local_sem.at[len(loads)]))

    for s in range(EARLY):
        load(hid.at[pl.ds(s * SPAN_LEN, SPAN_LEN)], gath.at[s, :, pl.ds(0, CHUNK)])
    for s in range(LATE):
        for h in range(2):
            load(
                hid.at[pl.ds((EARLY + s) * SPAN_LEN, SPAN_LEN), pl.ds(h * HALF, HALF)],
                hv.at[s, h],
            )
    hidden_loads = len(loads)
    for slot, (rel, other) in enumerate(
        [(0, 0), (0, 1), (3, 0), (1, 0), (3, 1), (1, 1), (2, 0), (2, 1)]
    ):
        core = c if other == 0 else 1 - c
        rows = pl.ds(pl.multiple_of((lax.rem(y + rel, 4) * 2 + core) * CHUNK, CHUNK), CHUNK)
        place = pl.ds(slot * CHUNK, CHUNK)
        load(wq_h.at[rows], wq.at[place])
        load(wkv_h.at[rows], wkv.at[place])
    load(pool_h, pool)
    for one in loads:
        one.start()

    barrier = pltpu.get_barrier_semaphore()
    for device in (up, down, sib):
        pl.semaphore_signal(barrier, inc=1, device_id=device, device_id_type=MESH)
    for peer in peers:
        pl.semaphore_signal(barrier, inc=1, device_id=(peer, tp), device_id_type=MESH)
    for one in loads[:hidden_loads]:
        one.wait()
    pl.semaphore_wait(barrier, 3 + REPS - 1)

    def remote(src, dst, send, recv, device):
        return pltpu.make_async_remote_copy(
            src_ref=src, dst_ref=dst, send_sem=send, recv_sem=recv,
            device_id=device, device_id_type=MESH,
        )

    def part(s, slot, first=0, count=SPAN_LEN):
        return gath.at[s, pl.ds(first, count), pl.ds(slot * CHUNK, CHUNK)]

    half = SPAN_LEN // 2

    def y_copy(kind, s):
        sems = (y_send.at[kind, s], y_recv.at[kind, s])
        if kind == 0:
            return remote(part(s, 0), part(s, 2), *sems, up)
        if kind == 1:
            return remote(part(s, 0), part(s, 3), *sems, down)
        if kind == 2:
            return remote(part(s, 0), part(s, 1), *sems, sib)
        if kind == 3:
            return remote(part(s, 2, 0, half), part(s, 6, 0, half), *sems, up)
        if kind == 4:
            return remote(part(s, 3, half, half), part(s, 6, half, half), *sems, down)
        if kind == 5:
            return remote(part(s, 2), part(s, 4), *sems, sib)
        if kind == 6:
            return remote(part(s, 3), part(s, 5), *sems, sib)
        return remote(part(s, 6), part(s, 7), *sems, sib)

    def near_send(s):
        for kind in (0, 1, 2):
            y_copy(kind, s).start()

    def exchange(phase, s, src, dst):
        for peer in peers:
            remote(
                src(peer), dst, x_send.at[phase, s], x_recv.at[phase, s], (peer, tp)
            ).start()

    def arrived(sem, ref):
        ref = ref.at[0, pl.ds(0, REPS - 1)]
        pltpu.make_async_copy(ref, ref, sem).wait()

    def sources(s):
        owners = [owner[r * STEPS + s] for r in range(REPS)]

        def of(o):
            found = jnp.int32(0)
            for r in range(1, REPS):
                found = jnp.where(owners[r] == o, r, found)
            return found

        return of

    def hidden_out(s):
        u = s - EARLY

        def src(j):
            return hv.at[u, j // 8, pl.ds(pl.multiple_of(lax.rem(j, 8) * 16, 16), 16)]

        exchange(4, s, src, rh.at[u, me])
        rh[u, me] = hv[u, me // 8, pl.ds(pl.multiple_of(lax.rem(me, 8) * 16, 16), 16)]

    def hidden_on(s):
        u = s - EARLY
        arrived(x_recv.at[4, s], rh)
        workh[...] = rh[u]
        of = sources(s)
        for o in range(REPS):
            sth[u, o] = workh[of(o)]
        rows = pl.ds(pl.multiple_of(lax.rem(me, 8) * 16, 16), 16)
        cols = pl.ds(pl.multiple_of(me // 8 * HALF, HALF), HALF)
        exchange(5, s, lambda o: sth.at[u, o], gath.at[s, rows, cols])
        for h in range(2):

            @pl.when(me // 8 == h)
            def _():
                gath[s, rows, h * HALF : (h + 1) * HALF] = sth[u, me]

    near_send(0)
    near_send(1)
    lax.fori_loop(EARLY, 2 * EARLY, lambda s, _: hidden_out(s), None)
    lax.fori_loop(EARLY, 2 * EARLY, lambda s, _: hidden_on(s), None)
    lax.fori_loop(2 * EARLY, 3 * EARLY, lambda s, _: hidden_out(s), None)
    for one in loads[hidden_loads:]:
        one.wait()

    lane = lax.broadcasted_iota(jnp.int32, (1, 128), 1)

    def project_near(s):
        slot = lax.rem(s, 2)
        x = gath[s, :, :NEAR]
        accq[slot] = jnp.dot(x, wq[:NEAR], preferred_element_type=F32)
        acck[slot] = jnp.dot(x, wkv[:NEAR], preferred_element_type=F32)

    def owned(s):
        return sources(s)(me) * STEPS + s

    def project_far(s):
        slot = lax.rem(s, 2)
        x = gath[s, :, NEAR:]
        query = accq[slot] + jnp.dot(x, wq[NEAR:], preferred_element_type=F32)
        keyval = acck[slot] + jnp.dot(x, wkv[NEAR:], preferred_element_type=F32)
        span = jnp.where(s < EARLY, me * STEPS + s, owned(s))
        angle = lens[span].astype(F32) * trig[2, :8]
        cos_p, sin_p = jnp.cos(angle)[:1], jnp.sin(angle)[:1]
        cos_t, sin_t = trig[0], trig[1]
        cosine = cos_p * cos_t - sin_p * sin_t
        sine = sin_p * cos_t + cos_p * sin_t
        sine = jnp.where(lane < HEAD_DIM // 2, -sine, sine)

        def rotate(v):
            return (v * cosine + pltpu.roll(v, HEAD_DIM // 2, 1) * sine).astype(BF)

        blocks = [rotate(query[:, h * 128 : (h + 1) * 128]) for h in range(GROUP)]
        blocks.append(rotate(keyval[:, :128]))
        blocks.append(keyval[:, 128:].astype(BF))
        return jnp.concatenate(blocks, axis=0).reshape(REPS, PIECE, 128)

    def attend(s):
        row = owned(s)
        length = lens[row]
        whole = r2[s].reshape(MSG, 128)
        fresh_k, fresh_v = whole[ROWS : ROWS + 128], whole[ROWS + 128 :]
        cache[s, :, :128] = fresh_k
        cache[s, :, 128:] = fresh_v
        nt = (((1,), (1,)), ((), ()))

        def page(j):
            return pool[pages[j, row]]

        position = lax.broadcasted_iota(jnp.int32, (1, 256), 1)
        t_key = lax.broadcasted_iota(jnp.int32, (BLOCK, 128), 1)
        t = lax.rem(lax.broadcasted_iota(jnp.int32, (BLOCK, 128), 0), SPAN_LEN)
        factor = SCALE * LOG2E
        for first in range(0, ROWS, BLOCK):
            q = whole[first : first + BLOCK]
            sc = lax.dot_general(q, fresh_k, nt, preferred_element_type=F32)
            sc = jnp.where(t_key <= t, sc, -jnp.inf)
            scores[:, PAGES * 128 :] = sc
            top = sc
            for j in range(0, PAGES, 2):
                keys = jnp.concatenate([page(j)[:, :128], page(j + 1)[:, :128]], axis=0)
                bias = jnp.where(position + j * 128 < length, 0.0, -jnp.inf)
                sc = lax.dot_general(q, keys, nt, preferred_element_type=F32) + bias
                scores[:, j * 128 : (j + 2) * 128] = sc
                top = jnp.maximum(top, jnp.maximum(sc[:, :128], sc[:, 128:]))
            highest = jnp.max(top, axis=1, keepdims=True) * factor
            w = jnp.exp2(scores[:, PAGES * 128 :] * factor - highest)
            total = w
            summed = jnp.dot(w.astype(BF), fresh_v, preferred_element_type=F32)
            for j in range(0, PAGES, 2):
                values = jnp.concatenate([page(j)[:, 128:], page(j + 1)[:, 128:]], axis=0)
                w = jnp.exp2(scores[:, j * 128 : (j + 2) * 128] * factor - highest)
                total = total + (w[:, :128] + w[:, 128:])
                summed = summed + jnp.dot(w.astype(BF), values, preferred_element_type=F32)
            total = jnp.sum(total, axis=1, keepdims=True)
            done = (summed / total).astype(BF).reshape(BLOCK // BACK, BACK, 128)
            om[s, first // BACK : (first + BLOCK) // BACK] = done

    def between(s, low, high):
        return pl.when((s >= low) & (s < high))

    def late_and_early(late, early, run):
        def one(n, carry):
            s = jnp.where(n == 0, late, early)

            @between(s, jnp.where(n == 0, EARLY, 0), jnp.where(n == 0, STEPS, EARLY))
            def _():
                run(s)

            return carry

        lax.fori_loop(0, 2, one, 0)

    def back_on(s):
        arrived(x_recv.at[2, s], r3)
        work3[...] = r3[s]
        for r in range(REPS):
            st4[s, r] = work3[owner[r * STEPS + s]]
        exchange(3, s, lambda r: st4.at[s, r], r4.at[s, me])
        r4[s, me] = st4[s, me]

    def finish(s):
        arrived(x_recv.at[3, s], r4)
        rows = pl.ds(pl.multiple_of(s * SPAN_LEN, SPAN_LEN), SPAN_LEN)
        whole = r4[s].reshape(ROWS, 128)
        for h in range(GROUP):
            out[rows, h * 128 : (h + 1) * 128] = whole[h * 128 : (h + 1) * 128]

    def work(s):
        @pl.when(s < EARLY)
        def _():
            arrived(x_recv.at[1, s], r1)

        attend(s)
        exchange(2, s, lambda j: om.at[s, j], r3.at[s, me])
        r3[s, me] = om[s, me]

    def step(it, carry):
        @between(it, 0, STEPS)
        def _():
            y_copy(0, it).wait_recv()
            y_copy(3, it).start()
            y_copy(5, it).start()
            y_copy(1, it).wait_recv()
            y_copy(4, it).start()
            y_copy(6, it).start()

        @between(it - 1, 0, STEPS)
        def _():
            y_copy(3, it - 1).wait_recv()
            y_copy(4, it - 1).wait_recv()
            y_copy(7, it - 1).start()

        late_and_early(it - 2, it - 5, back_on)

        @between(it - 2, 0, EARLY)
        def _():
            s = it - 2
            arrived(x_recv.at[0, s], r1)
            work1[...] = r1[s]
            of = sources(s)
            for o in range(REPS):
                st2[s, o] = work1[of(o)]
            exchange(1, s, lambda o: st2.at[s, o], r2.at[s, me])
            r2[s, me] = st2[s, me]

        @between(it + 4, 2 * EARLY, STEPS)
        def _():
            hidden_on(it + 4)

        @between(it + 6, 3 * EARLY, STEPS)
        def _():
            hidden_out(it + 6)

        @between(it - 1, 0, STEPS)
        def _():
            s = it - 1
            y_copy(7, s).wait_recv()
            whole = project_far(s)

            @pl.when(s < EARLY)
            def _():
                msg[s] = whole
                exchange(0, s, lambda j: msg.at[s, j], r1.at[s, me])
                r1[s, me] = msg[s, me]

            @pl.when(s >= EARLY)
            def _():
                r2[s] = whole

        @between(it + 2, EARLY, STEPS)
        def _():
            arrived(x_recv.at[5, it + 2], rh)
            near_send(it + 2)

        late_and_early(it - 1, it - 4, work)

        @between(it, 0, STEPS)
        def _():
            for kind in (2, 5, 6):
                y_copy(kind, it).wait_recv()
            project_near(it)

        late_and_early(it - 3, it - 6, finish)
        return carry

    lax.fori_loop(0, STEPS + 3, step, 0)

    def drain(s, carry):
        for kind in range(8):
            y_copy(kind, s).wait_send()
        arrived(x_send.at[2, s], om)
        arrived(x_send.at[3, s], st4)

        @pl.when(s < EARLY)
        def _():
            arrived(x_send.at[0, s], msg)
            arrived(x_send.at[1, s], st2)

        @pl.when(s >= EARLY)
        def _():
            arrived(x_send.at[4, s], rh)
            arrived(x_send.at[5, s], sth)

        return carry

    lax.fori_loop(0, STEPS, drain, 0)


def trig_tables():
    i = np.arange(64, dtype=np.float64)
    frequency = np.concatenate([ROPE_BASE ** (-2.0 * i / HEAD_DIM)] * 2)
    angle = np.arange(SPAN_LEN, dtype=np.float64)[:, None] * frequency[None, :]
    wide = np.broadcast_to(frequency[None, :], (SPAN_LEN, HEAD_DIM))
    return np.stack([np.cos(angle), np.sin(angle), wide]).astype(np.float32)


def body(hidden, w_query, w_keyval, kv_pool, prefix_len, owner, block_table):
    v = pltpu.VMEM
    dma = pltpu.SemaphoreType.DMA
    any_spec = pl.BlockSpec(memory_space=pl.ANY)
    vmem = pl.BlockSpec(memory_space=pltpu.VMEM)
    return pl.pallas_call(
        kernel,
        out_shape=(
            jax.ShapeDtypeStruct((STEPS * SPAN_LEN, GROUP * 128), BF),
            jax.ShapeDtypeStruct((STEPS, SPAN_LEN, 256), BF),
        ),
        in_specs=[pl.BlockSpec(memory_space=pltpu.SMEM)] * 3 + [any_spec] * 4 + [vmem],
        out_specs=(vmem, vmem),
        scratch_shapes=[
            v((STEPS, SPAN_LEN, 8 * CHUNK), BF),
            v((8 * CHUNK, GROUP * 128), BF),
            v((8 * CHUNK, 256), BF),
            v((128, 128, 256), BF),
            v((2, SPAN_LEN, GROUP * 128), F32),
            v((2, SPAN_LEN, 256), F32),
            v((LATE, 2, SPAN_LEN, HALF), BF),
            v((LATE, REPS, 16, HALF), BF),
            v((LATE, REPS, 16, HALF), BF),
            v((EARLY, REPS, PIECE, 128), BF),
            v((EARLY, REPS, PIECE, 128), BF),
            v((EARLY, REPS, PIECE, 128), BF),
            v((STEPS, REPS, PIECE, 128), BF),
            v((STEPS, REPS, BACK, 128), BF),
            v((STEPS, REPS, BACK, 128), BF),
            v((STEPS, REPS, BACK, 128), BF),
            v((STEPS, REPS, BACK, 128), BF),
            v((BLOCK, KEYS), F32),
            v((REPS, 16, HALF), BF),
            v((REPS, PIECE, 128), BF),
            v((REPS, BACK, 128), BF),
            dma((31,)),
            dma((8, STEPS)),
            dma((8, STEPS)),
            dma((6, STEPS)),
            dma((6, STEPS)),
        ],
        compiler_params=pltpu.CompilerParams(
            collective_id=0, has_side_effects=True, vmem_limit_bytes=62 * 1024 * 1024
        ),
        cost_estimate=pl.CostEstimate(
            flops=18_000_000_000, bytes_accessed=24_000_000, transcendentals=9_000_000
        ),
    )(prefix_len, owner, block_table.T, hidden, w_query, w_keyval, kv_pool, jnp.asarray(trig_tables()))


def solution(mesh):
    placed = (P("rep", "tp"), P(None, "tp"), P(None, "tp"), P("rep", None, "tp"), P(), P(), P())
    return jax.shard_map(
        body,
        mesh=mesh,
        in_specs=placed,
        out_specs=(P("rep", "tp"), P("rep", None, "tp")),
        check_vma=False,
    )
```

```python
import math

import jax
import jax.numpy as jnp
import numpy as np
from jax import lax
from jax.experimental import pallas as pl
from jax.experimental.pallas import tpu as pltpu
from jax.sharding import PartitionSpec as P

HEAD_DIM = 128
SPAN_LEN = 128
ROPE_BASE = 500000.0
MESH = pl.DeviceIdType.MESH
BF = jnp.bfloat16
F32 = jnp.float32

REPS = 16
STEPS = 8
PAGES = 16
GROUP = 4
ROWS = GROUP * SPAN_LEN
MSG = ROWS + 2 * SPAN_LEN
PIECE = MSG // REPS
BACK = ROWS // REPS
KEYS = PAGES * 128 + SPAN_LEN
CHUNK = 1024
NEAR = 6 * CHUNK
SCALE = 1.0 / math.sqrt(HEAD_DIM)
LOG2E = math.log2(math.e)

EARLY = 3
LATE = STEPS - EARLY
HALF = CHUNK // 2
BLOCK = 256
OFFSETS = [
    (2, 2), (2, 1), (1, 2), (2, 3), (3, 2), (1, 1), (3, 3), (1, 3), (3, 1),
    (0, 2), (2, 0), (0, 1), (1, 0), (0, 3), (3, 0),
]


def kernel(
    lens, owner, pages, hid, wq_h, wkv_h, pool_h, trig, out, cache,
    gath, wq, wkv, pool, accq, acck, hv, rh, sth, msg, r1, st2, r2, om, r3, st4, r4,
    scores, workh, work1, work3, outv, cachev,
    local_sem, out_sem, y_send, y_recv, x_send, x_recv,
):
    me = lax.axis_index("rep")
    tp = lax.axis_index("tp")
    y, c = tp // 2, lax.rem(tp, 2)
    up = (me, lax.rem(y + 1, 4) * 2 + c)
    down = (me, lax.rem(y + 3, 4) * 2 + c)
    sib = (me, y * 2 + 1 - c)
    peers = [
        lax.rem(me // 4 + dx, 4) * 4 + lax.rem(lax.rem(me, 4) + dz, 4) for dx, dz in OFFSETS
    ]

    loads = []

    def load(src, dst):
        loads.append(pltpu.make_async_copy(src, dst, local_sem.at[len(loads)]))

    for s in range(EARLY):
        load(hid.at[pl.ds(s * SPAN_LEN, SPAN_LEN)], gath.at[s, :, pl.ds(0, CHUNK)])
    for s in range(LATE):
        for h in range(2):
            load(
                hid.at[pl.ds((EARLY + s) * SPAN_LEN, SPAN_LEN), pl.ds(h * HALF, HALF)],
                hv.at[s, h],
            )
    hidden_loads = len(loads)
    for slot, (rel, other) in enumerate(
        [(0, 0), (0, 1), (3, 0), (1, 0), (3, 1), (1, 1), (2, 0), (2, 1)]
    ):
        core = c if other == 0 else 1 - c
        rows = pl.ds(pl.multiple_of((lax.rem(y + rel, 4) * 2 + core) * CHUNK, CHUNK), CHUNK)
        place = pl.ds(slot * CHUNK, CHUNK)
        load(wq_h.at[rows], wq.at[place])
        load(wkv_h.at[rows], wkv.at[place])
    load(pool_h, pool)
    for one in loads:
        one.start()

    barrier = pltpu.get_barrier_semaphore()
    for device in (up, down, sib):
        pl.semaphore_signal(barrier, inc=1, device_id=device, device_id_type=MESH)
    for peer in peers:
        pl.semaphore_signal(barrier, inc=1, device_id=(peer, tp), device_id_type=MESH)
    for one in loads[:hidden_loads]:
        one.wait()
    pl.semaphore_wait(barrier, 3 + REPS - 1)

    def remote(src, dst, send, recv, device):
        return pltpu.make_async_remote_copy(
            src_ref=src, dst_ref=dst, send_sem=send, recv_sem=recv,
            device_id=device, device_id_type=MESH,
        )

    def part(s, slot, first=0, count=SPAN_LEN):
        return gath.at[s, pl.ds(first, count), pl.ds(slot * CHUNK, CHUNK)]

    half = SPAN_LEN // 2

    def y_copy(kind, s):
        sems = (y_send.at[kind, s], y_recv.at[kind, s])
        if kind == 0:
            return remote(part(s, 0), part(s, 2), *sems, up)
        if kind == 1:
            return remote(part(s, 0), part(s, 3), *sems, down)
        if kind == 2:
            return remote(part(s, 0), part(s, 1), *sems, sib)
        if kind == 3:
            return remote(part(s, 2, 0, half), part(s, 6, 0, half), *sems, up)
        if kind == 4:
            return remote(part(s, 3, half, half), part(s, 6, half, half), *sems, down)
        if kind == 5:
            return remote(part(s, 2), part(s, 4), *sems, sib)
        if kind == 6:
            return remote(part(s, 3), part(s, 5), *sems, sib)
        return remote(part(s, 6), part(s, 7), *sems, sib)

    def near_send(s):
        for kind in (0, 1, 2):
            y_copy(kind, s).start()

    def exchange(phase, s, src, dst):
        for peer in peers:
            remote(
                src(peer), dst, x_send.at[phase, s], x_recv.at[phase, s], (peer, tp)
            ).start()

    def arrived(sem, ref):
        ref = ref.at[0, pl.ds(0, REPS - 1)]
        pltpu.make_async_copy(ref, ref, sem).wait()

    def sources(s):
        owners = [owner[r * STEPS + s] for r in range(REPS)]

        def of(o):
            found = jnp.int32(0)
            for r in range(1, REPS):
                found = jnp.where(owners[r] == o, r, found)
            return found

        return of

    def hidden_out(s):
        u = s - EARLY

        def src(j):
            return hv.at[u, j // 8, pl.ds(pl.multiple_of(lax.rem(j, 8) * 16, 16), 16)]

        exchange(4, s, src, rh.at[u, me])
        rh[u, me] = hv[u, me // 8, pl.ds(pl.multiple_of(lax.rem(me, 8) * 16, 16), 16)]

    def hidden_on(s):
        u = s - EARLY
        arrived(x_recv.at[4, s], rh)
        workh[...] = rh[u]
        of = sources(s)
        for o in range(REPS):
            sth[u, o] = workh[of(o)]
        rows = pl.ds(pl.multiple_of(lax.rem(me, 8) * 16, 16), 16)
        cols = pl.ds(pl.multiple_of(me // 8 * HALF, HALF), HALF)
        exchange(5, s, lambda o: sth.at[u, o], gath.at[s, rows, cols])
        for h in range(2):

            @pl.when(me // 8 == h)
            def _():
                gath[s, rows, h * HALF : (h + 1) * HALF] = sth[u, me]

    near_send(0)
    near_send(1)
    lax.fori_loop(EARLY, EARLY + 2, lambda s, _: hidden_out(s), None)
    for one in loads[hidden_loads:]:
        one.wait()

    lane = lax.broadcasted_iota(jnp.int32, (1, 128), 1)

    def project_near(s):
        slot = lax.rem(s, 2)
        x = gath[s, :, :NEAR]
        accq[slot] = jnp.dot(x, wq[:NEAR], preferred_element_type=F32)
        acck[slot] = jnp.dot(x, wkv[:NEAR], preferred_element_type=F32)

    def owned(s):
        return sources(s)(me) * STEPS + s

    def project_far(s):
        slot = lax.rem(s, 2)
        x = gath[s, :, NEAR:]
        query = accq[slot] + jnp.dot(x, wq[NEAR:], preferred_element_type=F32)
        keyval = acck[slot] + jnp.dot(x, wkv[NEAR:], preferred_element_type=F32)
        span = jnp.where(s < EARLY, me * STEPS + s, owned(s))
        angle = lens[span].astype(F32) * trig[2, :8]
        cos_p, sin_p = jnp.cos(angle)[:1], jnp.sin(angle)[:1]
        cos_t, sin_t = trig[0], trig[1]
        cosine = cos_p * cos_t - sin_p * sin_t
        sine = sin_p * cos_t + cos_p * sin_t
        sine = jnp.where(lane < HEAD_DIM // 2, -sine, sine)

        def rotate(v):
            return (v * cosine + pltpu.roll(v, HEAD_DIM // 2, 1) * sine).astype(BF)

        blocks = [rotate(query[:, h * 128 : (h + 1) * 128]) for h in range(GROUP)]
        blocks.append(rotate(keyval[:, :128]))
        blocks.append(keyval[:, 128:].astype(BF))
        return jnp.concatenate(blocks, axis=0).reshape(REPS, PIECE, 128)

    def cache_copy(s):
        return pltpu.make_async_copy(cachev.at[s], cache.at[s], out_sem.at[0, s])

    def out_copy(s):
        rows = pl.ds(pl.multiple_of(s * SPAN_LEN, SPAN_LEN), SPAN_LEN)
        return pltpu.make_async_copy(outv.at[s], out.at[rows], out_sem.at[1, s])

    def attend(s):
        row = owned(s)
        length = lens[row]
        whole = r2[s].reshape(MSG, 128)
        fresh_k, fresh_v = whole[ROWS : ROWS + 128], whole[ROWS + 128 :]
        cachev[s, :, :128] = fresh_k
        cachev[s, :, 128:] = fresh_v
        cache_copy(s).start()
        nt = (((1,), (1,)), ((), ()))

        def page(j):
            return pool[pages[j, row]]

        position = lax.broadcasted_iota(jnp.int32, (1, 256), 1)
        t_key = lax.broadcasted_iota(jnp.int32, (BLOCK, 128), 1)
        t = lax.rem(lax.broadcasted_iota(jnp.int32, (BLOCK, 128), 0), SPAN_LEN)
        factor = SCALE * LOG2E
        for first in range(0, ROWS, BLOCK):
            q = whole[first : first + BLOCK]
            sc = lax.dot_general(q, fresh_k, nt, preferred_element_type=F32)
            sc = jnp.where(t_key <= t, sc, -jnp.inf)
            scores[:, PAGES * 128 :] = sc
            top = sc
            for j in range(0, PAGES, 2):
                keys = jnp.concatenate([page(j)[:, :128], page(j + 1)[:, :128]], axis=0)
                bias = jnp.where(position + j * 128 < length, 0.0, -jnp.inf)
                sc = lax.dot_general(q, keys, nt, preferred_element_type=F32) + bias
                scores[:, j * 128 : (j + 2) * 128] = sc
                top = jnp.maximum(top, jnp.maximum(sc[:, :128], sc[:, 128:]))
            highest = jnp.max(top, axis=1, keepdims=True) * factor
            w = jnp.exp2(scores[:, PAGES * 128 :] * factor - highest)
            total = w
            summed = jnp.dot(w.astype(BF), fresh_v, preferred_element_type=F32)
            for j in range(0, PAGES, 2):
                values = jnp.concatenate([page(j)[:, 128:], page(j + 1)[:, 128:]], axis=0)
                w = jnp.exp2(scores[:, j * 128 : (j + 2) * 128] * factor - highest)
                total = total + (w[:, :128] + w[:, 128:])
                summed = summed + jnp.dot(w.astype(BF), values, preferred_element_type=F32)
            total = jnp.sum(total, axis=1, keepdims=True)
            done = (summed / total).astype(BF).reshape(BLOCK // BACK, BACK, 128)
            om[s, first // BACK : (first + BLOCK) // BACK] = done

    def between(s, low, high):
        return pl.when((s >= low) & (s < high))

    def late_and_early(late, early, run):
        def one(n, carry):
            s = jnp.where(n == 0, late, early)

            @between(s, jnp.where(n == 0, EARLY, 0), jnp.where(n == 0, STEPS, EARLY))
            def _():
                run(s)

            return carry

        lax.fori_loop(0, 2, one, 0)

    def back_on(s):
        arrived(x_recv.at[2, s], r3)
        work3[...] = r3[s]
        for r in range(REPS):
            st4[s, r] = work3[owner[r * STEPS + s]]
        exchange(3, s, lambda r: st4.at[s, r], r4.at[s, me])
        r4[s, me] = st4[s, me]

    def finish(s):
        arrived(x_recv.at[3, s], r4)
        whole = r4[s].reshape(ROWS, 128)
        for h in range(GROUP):
            outv[s, :, h * 128 : (h + 1) * 128] = whole[h * 128 : (h + 1) * 128]
        out_copy(s).start()

    def work(s):
        @pl.when(s < EARLY)
        def _():
            arrived(x_recv.at[1, s], r1)

        attend(s)
        exchange(2, s, lambda j: om.at[s, j], r3.at[s, me])
        r3[s, me] = om[s, me]

    def step(it, carry):
        @between(it, 0, STEPS)
        def _():
            y_copy(0, it).wait_recv()
            y_copy(3, it).start()
            y_copy(5, it).start()
            y_copy(1, it).wait_recv()
            y_copy(4, it).start()
            y_copy(6, it).start()

        @between(it - 1, 0, STEPS)
        def _():
            y_copy(3, it - 1).wait_recv()
            y_copy(4, it - 1).wait_recv()
            y_copy(7, it - 1).start()

        @between(it + 3, EARLY, STEPS)
        def _():
            hidden_on(it + 3)

        @between(it + 5, EARLY + 2, STEPS)
        def _():
            hidden_out(it + 5)

        @between(it - 1, 0, STEPS)
        def _():
            s = it - 1
            y_copy(7, s).wait_recv()
            whole = project_far(s)

            @pl.when(s < EARLY)
            def _():
                msg[s] = whole
                exchange(0, s, lambda j: msg.at[s, j], r1.at[s, me])
                r1[s, me] = msg[s, me]

            @pl.when(s >= EARLY)
            def _():
                r2[s] = whole

        @between(it + 2, 2, STEPS)
        def _():
            @pl.when(it + 2 >= EARLY)
            def _():
                arrived(x_recv.at[5, it + 2], rh)

            near_send(it + 2)

        late_and_early(it - 1, it - 4, work)
        late_and_early(it - 2, it - 5, back_on)

        @between(it - 2, 0, EARLY)
        def _():
            s = it - 2
            arrived(x_recv.at[0, s], r1)
            work1[...] = r1[s]
            of = sources(s)
            for o in range(REPS):
                st2[s, o] = work1[of(o)]
            exchange(1, s, lambda o: st2.at[s, o], r2.at[s, me])
            r2[s, me] = st2[s, me]

        @between(it, 0, STEPS)
        def _():
            for kind in (2, 5, 6):
                y_copy(kind, it).wait_recv()
            project_near(it)

        late_and_early(it - 3, it - 6, finish)
        return carry

    lax.fori_loop(0, STEPS + 3, step, 0)

    def drain(s, carry):
        for kind in range(8):
            y_copy(kind, s).wait_send()
        cache_copy(s).wait()
        out_copy(s).wait()
        arrived(x_send.at[2, s], om)
        arrived(x_send.at[3, s], st4)

        @pl.when(s < EARLY)
        def _():
            arrived(x_send.at[0, s], msg)
            arrived(x_send.at[1, s], st2)

        @pl.when(s >= EARLY)
        def _():
            arrived(x_send.at[4, s], rh)
            arrived(x_send.at[5, s], sth)

        return carry

    lax.fori_loop(0, STEPS, drain, 0)


def hand_over(a, b, out, cache, a_held, b_held, sem):
    parts = []
    for s in range(0, STEPS, 2):
        rows = pl.ds(s * SPAN_LEN, 2 * SPAN_LEN)
        parts.append((a.at[rows], a_held.at[rows], out.at[rows]))
        spans = pl.ds(s, 2)
        parts.append((b.at[spans], b_held.at[spans], cache.at[spans]))
    first = [pltpu.make_async_copy(p[0], p[1], sem.at[0, i]) for i, p in enumerate(parts)]
    second = [pltpu.make_async_copy(p[1], p[2], sem.at[1, i]) for i, p in enumerate(parts)]
    for copy in first:
        copy.start()
    for one, two in zip(first, second):
        one.wait()
        two.start()
    for copy in second:
        copy.wait()


def trig_tables():
    i = np.arange(64, dtype=np.float64)
    frequency = np.concatenate([ROPE_BASE ** (-2.0 * i / HEAD_DIM)] * 2)
    angle = np.arange(SPAN_LEN, dtype=np.float64)[:, None] * frequency[None, :]
    wide = np.broadcast_to(frequency[None, :], (SPAN_LEN, HEAD_DIM))
    return np.stack([np.cos(angle), np.sin(angle), wide]).astype(np.float32)


def body(hidden, w_query, w_keyval, kv_pool, prefix_len, owner, block_table):
    v = pltpu.VMEM
    dma = pltpu.SemaphoreType.DMA
    any_spec = pl.BlockSpec(memory_space=pl.ANY)
    vmem = pl.BlockSpec(memory_space=pltpu.VMEM)
    shapes = (
        jax.ShapeDtypeStruct((STEPS * SPAN_LEN, GROUP * 128), BF),
        jax.ShapeDtypeStruct((STEPS, SPAN_LEN, 256), BF),
    )
    results = pl.pallas_call(
        kernel,
        out_shape=shapes,
        in_specs=[pl.BlockSpec(memory_space=pltpu.SMEM)] * 3 + [any_spec] * 4 + [vmem],
        out_specs=(any_spec, any_spec),
        scratch_shapes=[
            v((STEPS, SPAN_LEN, 8 * CHUNK), BF),
            v((8 * CHUNK, GROUP * 128), BF),
            v((8 * CHUNK, 256), BF),
            v((128, 128, 256), BF),
            v((2, SPAN_LEN, GROUP * 128), F32),
            v((2, SPAN_LEN, 256), F32),
            v((LATE, 2, SPAN_LEN, HALF), BF),
            v((LATE, REPS, 16, HALF), BF),
            v((LATE, REPS, 16, HALF), BF),
            v((EARLY, REPS, PIECE, 128), BF),
            v((EARLY, REPS, PIECE, 128), BF),
            v((EARLY, REPS, PIECE, 128), BF),
            v((STEPS, REPS, PIECE, 128), BF),
            v((STEPS, REPS, BACK, 128), BF),
            v((STEPS, REPS, BACK, 128), BF),
            v((STEPS, REPS, BACK, 128), BF),
            v((STEPS, REPS, BACK, 128), BF),
            v((BLOCK, KEYS), F32),
            v((REPS, 16, HALF), BF),
            v((REPS, PIECE, 128), BF),
            v((REPS, BACK, 128), BF),
            v((STEPS, SPAN_LEN, GROUP * 128), BF),
            v((STEPS, SPAN_LEN, 256), BF),
            dma((EARLY + 2 * LATE + 17,)),
            dma((2, STEPS)),
            dma((8, STEPS)),
            dma((8, STEPS)),
            dma((6, STEPS)),
            dma((6, STEPS)),
        ],
        compiler_params=pltpu.CompilerParams(
            collective_id=0, has_side_effects=True, vmem_limit_bytes=62 * 1024 * 1024
        ),
        cost_estimate=pl.CostEstimate(
            flops=18_000_000_000, bytes_accessed=24_000_000, transcendentals=9_000_000
        ),
    )(prefix_len, owner, block_table.T, hidden, w_query, w_keyval, kv_pool, jnp.asarray(trig_tables()))
    return pl.pallas_call(
        hand_over,
        out_shape=shapes,
        in_specs=[any_spec] * 2,
        out_specs=(any_spec, any_spec),
        scratch_shapes=[v(shapes[0].shape, BF), v(shapes[1].shape, BF), dma((2, STEPS))],
    )(*results)


def solution(mesh):
    placed = (P("rep", "tp"), P(None, "tp"), P(None, "tp"), P("rep", None, "tp"), P(), P(), P())
    return jax.shard_map(
        body,
        mesh=mesh,
        in_specs=placed,
        out_specs=(P("rep", "tp"), P("rep", None, "tp")),
        check_vma=False,
    )
```

```python
import math

import jax
import jax.numpy as jnp
import numpy as np
from jax import lax
from jax.experimental import pallas as pl
from jax.experimental.pallas import tpu as pltpu
from jax.sharding import PartitionSpec as P

HEAD_DIM = 128
SPAN_LEN = 128
ROPE_BASE = 500000.0
MESH = pl.DeviceIdType.MESH
BF = jnp.bfloat16
F32 = jnp.float32

REPS = 16
STEPS = 8
PAGES = 16
GROUP = 4
ROWS = GROUP * SPAN_LEN
MSG = ROWS + 2 * SPAN_LEN
PIECE = MSG // REPS
BACK = ROWS // REPS
KEYS = PAGES * 128 + SPAN_LEN
CHUNK = 1024
NEAR = 6 * CHUNK
SCALE = 1.0 / math.sqrt(HEAD_DIM)
LOG2E = math.log2(math.e)

EARLY = 3
LATE = STEPS - EARLY
HALF = CHUNK // 2
BLOCK = 256
OFFSETS = [
    (2, 2), (2, 1), (1, 2), (2, 3), (3, 2), (1, 1), (3, 3), (1, 3), (3, 1),
    (0, 2), (2, 0), (0, 1), (1, 0), (0, 3), (3, 0),
]


def kernel(
    lens, owner, pages, hid, wq_h, wkv_h, pool_h, trig, back, cache,
    gath, wq, wkv, pool, accq, acck, hv, rh, sth, msg, r1, st2, r2, om, r3, st4,
    scores, workh, work1, work3, cachev,
    local_sem, out_sem, hello, y_send, y_recv, x_send, x_recv,
):
    me = lax.axis_index("rep")
    tp = lax.axis_index("tp")
    y, c = tp // 2, lax.rem(tp, 2)
    up = (me, lax.rem(y + 1, 4) * 2 + c)
    down = (me, lax.rem(y + 3, 4) * 2 + c)
    sib = (me, y * 2 + 1 - c)
    peers = [
        lax.rem(me // 4 + dx, 4) * 4 + lax.rem(lax.rem(me, 4) + dz, 4) for dx, dz in OFFSETS
    ]

    loads = []

    def load(src, dst):
        loads.append(pltpu.make_async_copy(src, dst, local_sem.at[len(loads)]))

    for s in range(EARLY):
        load(hid.at[pl.ds(s * SPAN_LEN, SPAN_LEN)], gath.at[s, :, pl.ds(0, CHUNK)])
    for s in range(LATE):
        for h in range(2):
            load(
                hid.at[pl.ds((EARLY + s) * SPAN_LEN, SPAN_LEN), pl.ds(h * HALF, HALF)],
                hv.at[s, h],
            )
    hidden_loads = len(loads)
    for slot, (rel, other) in enumerate(
        [(0, 0), (0, 1), (3, 0), (1, 0), (3, 1), (1, 1), (2, 0), (2, 1)]
    ):
        core = c if other == 0 else 1 - c
        rows = pl.ds(pl.multiple_of((lax.rem(y + rel, 4) * 2 + core) * CHUNK, CHUNK), CHUNK)
        place = pl.ds(slot * CHUNK, CHUNK)
        load(wq_h.at[rows], wq.at[place])
        load(wkv_h.at[rows], wkv.at[place])
    load(pool_h, pool)
    for one in loads:
        one.start()

    def along(dx, dz):
        return (lax.rem(me // 4 + dx, 4) * 4 + lax.rem(lax.rem(me, 4) + dz, 4), tp)

    barrier = pltpu.get_barrier_semaphore()
    for device in (up, down, sib, along(1, 0), along(3, 0), along(0, 1), along(0, 3)):
        pl.semaphore_signal(barrier, inc=1, device_id=device, device_id_type=MESH)
    for one in loads[:hidden_loads]:
        one.wait()
    pl.semaphore_wait(barrier, 7)

    def remote(src, dst, send, recv, device):
        return pltpu.make_async_remote_copy(
            src_ref=src, dst_ref=dst, send_sem=send, recv_sem=recv,
            device_id=device, device_id_type=MESH,
        )

    def part(s, slot, first=0, count=SPAN_LEN):
        return gath.at[s, pl.ds(first, count), pl.ds(slot * CHUNK, CHUNK)]

    half = SPAN_LEN // 2

    def y_copy(kind, s):
        sems = (y_send.at[kind, s], y_recv.at[kind, s])
        if kind == 0:
            return remote(part(s, 0), part(s, 2), *sems, up)
        if kind == 1:
            return remote(part(s, 0), part(s, 3), *sems, down)
        if kind == 2:
            return remote(part(s, 0), part(s, 1), *sems, sib)
        if kind == 3:
            return remote(part(s, 2, 0, half), part(s, 6, 0, half), *sems, up)
        if kind == 4:
            return remote(part(s, 3, half, half), part(s, 6, half, half), *sems, down)
        if kind == 5:
            return remote(part(s, 2), part(s, 4), *sems, sib)
        if kind == 6:
            return remote(part(s, 3), part(s, 5), *sems, sib)
        return remote(part(s, 6), part(s, 7), *sems, sib)

    def near_send(s):
        for kind in (0, 1, 2):
            y_copy(kind, s).start()

    def exchange(phase, s, src, dst):
        for peer in peers:
            remote(
                src(peer), dst, x_send.at[phase, s], x_recv.at[phase, s], (peer, tp)
            ).start()

    def arrived(sem, ref):
        ref = ref.at[0, pl.ds(0, REPS - 1)]
        pltpu.make_async_copy(ref, ref, sem).wait()

    def sources(s):
        owners = [owner[r * STEPS + s] for r in range(REPS)]

        def of(o):
            found = jnp.int32(0)
            for r in range(1, REPS):
                found = jnp.where(owners[r] == o, r, found)
            return found

        return of

    def hidden_out(s):
        u = s - EARLY

        def src(j):
            return hv.at[u, j // 8, pl.ds(pl.multiple_of(lax.rem(j, 8) * 16, 16), 16)]

        exchange(4, s, src, rh.at[u, me])
        rh[u, me] = hv[u, me // 8, pl.ds(pl.multiple_of(lax.rem(me, 8) * 16, 16), 16)]

    def hidden_on(s):
        u = s - EARLY
        arrived(x_recv.at[4, s], rh)
        workh[...] = rh[u]
        of = sources(s)
        for o in range(REPS):
            sth[u, o] = workh[of(o)]
        rows = pl.ds(pl.multiple_of(lax.rem(me, 8) * 16, 16), 16)
        cols = pl.ds(pl.multiple_of(me // 8 * HALF, HALF), HALF)
        exchange(5, s, lambda o: sth.at[u, o], gath.at[s, rows, cols])
        for h in range(2):

            @pl.when(me // 8 == h)
            def _():
                gath[s, rows, h * HALF : (h + 1) * HALF] = sth[u, me]

    near_send(0)
    near_send(1)
    for n, (dx, dz) in enumerate([(1, 0), (0, 1), (0, 1)]):
        for device in (along(dx, dz), along(3 * dx, 3 * dz)):
            pl.semaphore_signal(hello.at[n], inc=1, device_id=device, device_id_type=MESH)
        pl.semaphore_wait(hello.at[n], 2)
    lax.fori_loop(EARLY, EARLY + 2, lambda s, _: hidden_out(s), None)
    for one in loads[hidden_loads:]:
        one.wait()

    lane = lax.broadcasted_iota(jnp.int32, (1, 128), 1)

    def project_near(s):
        slot = lax.rem(s, 2)
        x = gath[s, :, :NEAR]
        accq[slot] = jnp.dot(x, wq[:NEAR], preferred_element_type=F32)
        acck[slot] = jnp.dot(x, wkv[:NEAR], preferred_element_type=F32)

    def owned(s):
        return sources(s)(me) * STEPS + s

    def project_far(s):
        slot = lax.rem(s, 2)
        x = gath[s, :, NEAR:]
        query = accq[slot] + jnp.dot(x, wq[NEAR:], preferred_element_type=F32)
        keyval = acck[slot] + jnp.dot(x, wkv[NEAR:], preferred_element_type=F32)
        span = jnp.where(s < EARLY, me * STEPS + s, owned(s))
        angle = lens[span].astype(F32) * trig[2, :8]
        cos_p, sin_p = jnp.cos(angle)[:1], jnp.sin(angle)[:1]
        cos_t, sin_t = trig[0], trig[1]
        cosine = cos_p * cos_t - sin_p * sin_t
        sine = sin_p * cos_t + cos_p * sin_t
        sine = jnp.where(lane < HEAD_DIM // 2, -sine, sine)

        def rotate(v):
            return (v * cosine + pltpu.roll(v, HEAD_DIM // 2, 1) * sine).astype(BF)

        blocks = [rotate(query[:, h * 128 : (h + 1) * 128]) for h in range(GROUP)]
        blocks.append(rotate(keyval[:, :128]))
        blocks.append(keyval[:, 128:].astype(BF))
        return jnp.concatenate(blocks, axis=0).reshape(REPS, PIECE, 128)

    def cache_copy(s):
        return pltpu.make_async_copy(cachev.at[s], cache.at[s], out_sem.at[0, s])

    def place(s):
        rows = pl.ds(pl.multiple_of(s * SPAN_LEN + lax.rem(me, 4) * BACK, BACK), BACK)
        return back.at[rows, pl.ds(pl.multiple_of(me // 4 * 128, 128), 128)]

    def own_copy(s):
        return pltpu.make_async_copy(st4.at[s, me], place(s), out_sem.at[1, s])

    def attend(s):
        row = owned(s)
        length = lens[row]
        whole = r2[s].reshape(MSG, 128)
        fresh_k, fresh_v = whole[ROWS : ROWS + 128], whole[ROWS + 128 :]
        cachev[s, :, :128] = fresh_k
        cachev[s, :, 128:] = fresh_v
        cache_copy(s).start()
        nt = (((1,), (1,)), ((), ()))

        def page(j):
            return pool[pages[j, row]]

        position = lax.broadcasted_iota(jnp.int32, (1, 256), 1)
        t_key = lax.broadcasted_iota(jnp.int32, (BLOCK, 128), 1)
        t = lax.rem(lax.broadcasted_iota(jnp.int32, (BLOCK, 128), 0), SPAN_LEN)
        factor = SCALE * LOG2E
        for first in range(0, ROWS, BLOCK):
            q = whole[first : first + BLOCK]
            sc = lax.dot_general(q, fresh_k, nt, preferred_element_type=F32)
            sc = jnp.where(t_key <= t, sc, -jnp.inf)
            scores[:, PAGES * 128 :] = sc
            top = sc
            for j in range(0, PAGES, 2):
                keys = jnp.concatenate([page(j)[:, :128], page(j + 1)[:, :128]], axis=0)
                bias = jnp.where(position + j * 128 < length, 0.0, -jnp.inf)
                sc = lax.dot_general(q, keys, nt, preferred_element_type=F32) + bias
                scores[:, j * 128 : (j + 2) * 128] = sc
                top = jnp.maximum(top, jnp.maximum(sc[:, :128], sc[:, 128:]))
            highest = jnp.max(top, axis=1, keepdims=True) * factor
            w = jnp.exp2(scores[:, PAGES * 128 :] * factor - highest)
            total = w
            summed = jnp.dot(w.astype(BF), fresh_v, preferred_element_type=F32)
            for j in range(0, PAGES, 2):
                values = jnp.concatenate([page(j)[:, 128:], page(j + 1)[:, 128:]], axis=0)
                w = jnp.exp2(scores[:, j * 128 : (j + 2) * 128] * factor - highest)
                total = total + (w[:, :128] + w[:, 128:])
                summed = summed + jnp.dot(w.astype(BF), values, preferred_element_type=F32)
            total = jnp.sum(total, axis=1, keepdims=True)
            done = (summed / total).astype(BF).reshape(BLOCK // BACK, BACK, 128)
            om[s, first // BACK : (first + BLOCK) // BACK] = done

    def between(s, low, high):
        return pl.when((s >= low) & (s < high))

    def late_and_early(late, early, run):
        def one(n, carry):
            s = jnp.where(n == 0, late, early)

            @between(s, jnp.where(n == 0, EARLY, 0), jnp.where(n == 0, STEPS, EARLY))
            def _():
                run(s)

            return carry

        lax.fori_loop(0, 2, one, 0)

    def back_on(s):
        arrived(x_recv.at[2, s], r3)
        work3[...] = r3[s]
        for r in range(REPS):
            st4[s, r] = work3[owner[r * STEPS + s]]
        exchange(3, s, lambda r: st4.at[s, r], place(s))
        own_copy(s).start()

    def settle(s):
        for kind in range(8):
            y_copy(kind, s).wait_send()
        cache_copy(s).wait()
        arrived(x_send.at[2, s], om)

        @pl.when(s < EARLY)
        def _():
            arrived(x_send.at[0, s], msg)
            arrived(x_send.at[1, s], st2)

        @pl.when(s >= EARLY)
        def _():
            arrived(x_send.at[4, s], rh)
            arrived(x_send.at[5, s], sth)

    def finish(s):
        own_copy(s).wait()
        arrived(x_send.at[3, s], st4)
        arrived(x_recv.at[3, s], st4)

    def work(s):
        @pl.when(s < EARLY)
        def _():
            arrived(x_recv.at[1, s], r1)

        attend(s)
        exchange(2, s, lambda j: om.at[s, j], r3.at[s, me])
        r3[s, me] = om[s, me]

    def far_on(s):
        y_copy(3, s).wait_recv()
        y_copy(4, s).wait_recv()
        y_copy(7, s).start()

    def step(it, carry):
        @between(it, 0, STEPS)
        def _():
            y_copy(0, it).wait_recv()
            y_copy(3, it).start()
            y_copy(5, it).start()
            y_copy(1, it).wait_recv()
            y_copy(4, it).start()
            y_copy(6, it).start()

        @between(it - 1, 0, STEPS - 1)
        def _():
            far_on(it - 1)

        @between(it + 3, EARLY, STEPS)
        def _():
            hidden_on(it + 3)

        @between(it + 5, EARLY + 2, STEPS)
        def _():
            hidden_out(it + 5)

        @between(it - 1, 0, STEPS)
        def _():
            s = it - 1
            y_copy(7, s).wait_recv()
            whole = project_far(s)

            @pl.when(s < EARLY)
            def _():
                msg[s] = whole
                exchange(0, s, lambda j: msg.at[s, j], r1.at[s, me])
                r1[s, me] = msg[s, me]

            @pl.when(s >= EARLY)
            def _():
                r2[s] = whole

        @between(it + 2, 2, STEPS)
        def _():
            @pl.when(it + 2 >= EARLY)
            def _():
                arrived(x_recv.at[5, it + 2], rh)

            near_send(it + 2)

        late_and_early(it - 1, it - 4, work)
        @pl.when(it == STEPS - 1)
        def _():
            far_on(it)

        late_and_early(it - 2, it - 5, back_on)

        @between(it - 2, 0, EARLY)
        def _():
            s = it - 2
            arrived(x_recv.at[0, s], r1)
            work1[...] = r1[s]
            of = sources(s)
            for o in range(REPS):
                st2[s, o] = work1[of(o)]
            exchange(1, s, lambda o: st2.at[s, o], r2.at[s, me])
            r2[s, me] = st2[s, me]

        @between(it, 0, STEPS)
        def _():
            for kind in (2, 5, 6):
                y_copy(kind, it).wait_recv()
            project_near(it)

        late_and_early(it - 2, it - 6, settle)
        late_and_early(it - 3, it - 7, finish)
        return carry

    lax.fori_loop(0, STEPS + 3, step, 0)


def hand_over(back, fresh, out, cache, out_held, cache_held, sem):
    parts = []
    for s in range(0, STEPS, 2):
        rows = pl.ds(s * SPAN_LEN, 2 * SPAN_LEN)
        parts.append((back.at[rows], out_held.at[rows], out.at[rows]))
    for s in range(0, STEPS, 4):
        spans = pl.ds(s, 4)
        parts.append((fresh.at[spans], cache_held.at[spans], cache.at[spans]))
    first = [pltpu.make_async_copy(p[0], p[1], sem.at[0, i]) for i, p in enumerate(parts)]
    second = [pltpu.make_async_copy(p[1], p[2], sem.at[1, i]) for i, p in enumerate(parts)]
    for copy in first:
        copy.start()
    for one, two in zip(first, second):
        one.wait()
        two.start()
    for copy in second:
        copy.wait()


def trig_tables():
    i = np.arange(64, dtype=np.float64)
    frequency = np.concatenate([ROPE_BASE ** (-2.0 * i / HEAD_DIM)] * 2)
    angle = np.arange(SPAN_LEN, dtype=np.float64)[:, None] * frequency[None, :]
    wide = np.broadcast_to(frequency[None, :], (SPAN_LEN, HEAD_DIM))
    return np.stack([np.cos(angle), np.sin(angle), wide]).astype(np.float32)


def body(hidden, w_query, w_keyval, kv_pool, prefix_len, owner, block_table):
    v = pltpu.VMEM
    dma = pltpu.SemaphoreType.DMA
    any_spec = pl.BlockSpec(memory_space=pl.ANY)
    vmem = pl.BlockSpec(memory_space=pltpu.VMEM)
    shapes = (
        jax.ShapeDtypeStruct((STEPS * SPAN_LEN, GROUP * 128), BF),
        jax.ShapeDtypeStruct((STEPS, SPAN_LEN, 256), BF),
    )
    results = pl.pallas_call(
        kernel,
        out_shape=shapes,
        in_specs=[pl.BlockSpec(memory_space=pltpu.SMEM)] * 3 + [any_spec] * 4 + [vmem],
        out_specs=(any_spec, any_spec),
        scratch_shapes=[
            v((STEPS, SPAN_LEN, 8 * CHUNK), BF),
            v((8 * CHUNK, GROUP * 128), BF),
            v((8 * CHUNK, 256), BF),
            v((128, 128, 256), BF),
            v((2, SPAN_LEN, GROUP * 128), F32),
            v((2, SPAN_LEN, 256), F32),
            v((LATE, 2, SPAN_LEN, HALF), BF),
            v((LATE, REPS, 16, HALF), BF),
            v((LATE, REPS, 16, HALF), BF),
            v((EARLY, REPS, PIECE, 128), BF),
            v((EARLY, REPS, PIECE, 128), BF),
            v((EARLY, REPS, PIECE, 128), BF),
            v((STEPS, REPS, PIECE, 128), BF),
            v((STEPS, REPS, BACK, 128), BF),
            v((STEPS, REPS, BACK, 128), BF),
            v((STEPS, REPS, BACK, 128), BF),
            v((BLOCK, KEYS), F32),
            v((REPS, 16, HALF), BF),
            v((REPS, PIECE, 128), BF),
            v((REPS, BACK, 128), BF),
            v((STEPS, SPAN_LEN, 256), BF),
            dma((EARLY + 2 * LATE + 17,)),
            dma((2, STEPS)),
            pltpu.SemaphoreType.REGULAR((3,)),
            dma((8, STEPS)),
            dma((8, STEPS)),
            dma((6, STEPS)),
            dma((6, STEPS)),
        ],
        compiler_params=pltpu.CompilerParams(
            collective_id=0, has_side_effects=True, vmem_limit_bytes=62 * 1024 * 1024
        ),
        cost_estimate=pl.CostEstimate(
            flops=18_000_000_000, bytes_accessed=24_000_000, transcendentals=9_000_000
        ),
    )(prefix_len, owner, block_table.T, hidden, w_query, w_keyval, kv_pool, jnp.asarray(trig_tables()))
    return pl.pallas_call(
        hand_over,
        out_shape=shapes,
        in_specs=[any_spec] * 2,
        out_specs=(any_spec, any_spec),
        scratch_shapes=[v(shapes[0].shape, BF), v(shapes[1].shape, BF), dma((2, STEPS))],
    )(*results)


def solution(mesh):
    placed = (P("rep", "tp"), P(None, "tp"), P(None, "tp"), P("rep", None, "tp"), P(), P(), P())
    return jax.shard_map(
        body,
        mesh=mesh,
        in_specs=placed,
        out_specs=(P("rep", "tp"), P("rep", None, "tp")),
        check_vma=False,
    )
```

```python
import math

import jax
import jax.numpy as jnp
import numpy as np
from jax import lax
from jax.experimental import pallas as pl
from jax.experimental.pallas import tpu as pltpu
from jax.sharding import PartitionSpec as P

HEAD_DIM = 128
SPAN_LEN = 128
ROPE_BASE = 500000.0
MESH = pl.DeviceIdType.MESH
BF = jnp.bfloat16
F32 = jnp.float32

REPS = 16
STEPS = 8
PAGES = 16
GROUP = 4
ROWS = GROUP * SPAN_LEN
MSG = ROWS + 2 * SPAN_LEN
PIECE = MSG // REPS
BACK = ROWS // REPS
KEYS = PAGES * 128 + SPAN_LEN
CHUNK = 1024
NEAR = 6 * CHUNK
SCALE = 1.0 / math.sqrt(HEAD_DIM)
LOG2E = math.log2(math.e)

EARLY = 3
LATE = STEPS - EARLY
HALF = CHUNK // 2
BLOCK = 256
OFFSETS = [
    (2, 2), (2, 1), (1, 2), (2, 3), (3, 2), (1, 1), (3, 3), (1, 3), (3, 1),
    (0, 2), (2, 0), (0, 1), (1, 0), (0, 3), (3, 0),
]


def kernel(
    lens, owner, pages, hid, wq_h, wkv_h, pool_h, trig, back, cache,
    gath, wq, wkv, pool, accq, acck, hv, rh, sth, msg, r1, st2, r2, om, r3, st4,
    scores, workh, work1, work3, cachev,
    local_sem, out_sem, hello, y_send, y_recv, x_send, x_recv,
):
    me = lax.axis_index("rep")
    tp = lax.axis_index("tp")
    y, c = tp // 2, lax.rem(tp, 2)
    up = (me, lax.rem(y + 1, 4) * 2 + c)
    down = (me, lax.rem(y + 3, 4) * 2 + c)
    sib = (me, y * 2 + 1 - c)
    peers = [
        lax.rem(me // 4 + dx, 4) * 4 + lax.rem(lax.rem(me, 4) + dz, 4) for dx, dz in OFFSETS
    ]

    loads = []

    def load(src, dst):
        loads.append(pltpu.make_async_copy(src, dst, local_sem.at[len(loads)]))

    for s in range(EARLY):
        load(hid.at[pl.ds(s * SPAN_LEN, SPAN_LEN)], gath.at[s, :, pl.ds(0, CHUNK)])
    for s in range(LATE):
        for h in range(2):
            load(
                hid.at[pl.ds((EARLY + s) * SPAN_LEN, SPAN_LEN), pl.ds(h * HALF, HALF)],
                hv.at[s, h],
            )
    hidden_loads = len(loads)
    for slot, (rel, other) in enumerate(
        [(0, 0), (0, 1), (3, 0), (1, 0), (3, 1), (1, 1), (2, 0), (2, 1)]
    ):
        core = c if other == 0 else 1 - c
        rows = pl.ds(pl.multiple_of((lax.rem(y + rel, 4) * 2 + core) * CHUNK, CHUNK), CHUNK)
        place = pl.ds(slot * CHUNK, CHUNK)
        load(wq_h.at[rows], wq.at[place])
        load(wkv_h.at[rows], wkv.at[place])
    load(pool_h, pool)
    for one in loads:
        one.start()

    def along(dx, dz):
        return (lax.rem(me // 4 + dx, 4) * 4 + lax.rem(lax.rem(me, 4) + dz, 4), tp)

    barrier = pltpu.get_barrier_semaphore()
    for device in (up, down, sib, along(1, 0), along(3, 0), along(0, 1), along(0, 3)):
        pl.semaphore_signal(barrier, inc=1, device_id=device, device_id_type=MESH)
    for one in loads[:hidden_loads]:
        one.wait()
    pl.semaphore_wait(barrier, 7)

    def remote(src, dst, send, recv, device):
        return pltpu.make_async_remote_copy(
            src_ref=src, dst_ref=dst, send_sem=send, recv_sem=recv,
            device_id=device, device_id_type=MESH,
        )

    def part(s, slot, first=0, count=SPAN_LEN):
        return gath.at[s, pl.ds(first, count), pl.ds(slot * CHUNK, CHUNK)]

    half = SPAN_LEN // 2

    def y_copy(kind, s):
        sems = (y_send.at[kind, s], y_recv.at[kind, s])
        if kind == 0:
            return remote(part(s, 0), part(s, 2), *sems, up)
        if kind == 1:
            return remote(part(s, 0), part(s, 3), *sems, down)
        if kind == 2:
            return remote(part(s, 0), part(s, 1), *sems, sib)
        if kind == 3:
            return remote(part(s, 2, 0, half), part(s, 6, 0, half), *sems, up)
        if kind == 4:
            return remote(part(s, 3, half, half), part(s, 6, half, half), *sems, down)
        if kind == 5:
            return remote(part(s, 2), part(s, 4), *sems, sib)
        if kind == 6:
            return remote(part(s, 3), part(s, 5), *sems, sib)
        return remote(part(s, 6), part(s, 7), *sems, sib)

    def near_send(s):
        for kind in (0, 1, 2):
            y_copy(kind, s).start()

    def exchange(phase, s, src, dst):
        for peer in peers:
            remote(
                src(peer), dst, x_send.at[phase, s], x_recv.at[phase, s], (peer, tp)
            ).start()

    def arrived(sem, ref):
        ref = ref.at[0, pl.ds(0, REPS - 1)]
        pltpu.make_async_copy(ref, ref, sem).wait()

    def sources(s):
        owners = [owner[r * STEPS + s] for r in range(REPS)]

        def of(o):
            found = jnp.int32(0)
            for r in range(1, REPS):
                found = jnp.where(owners[r] == o, r, found)
            return found

        return of

    def hidden_out(s):
        u = s - EARLY

        def src(j):
            return hv.at[u, j // 8, pl.ds(pl.multiple_of(lax.rem(j, 8) * 16, 16), 16)]

        exchange(4, s, src, rh.at[u, me])
        rh[u, me] = hv[u, me // 8, pl.ds(pl.multiple_of(lax.rem(me, 8) * 16, 16), 16)]

    def hidden_on(s):
        u = s - EARLY
        arrived(x_recv.at[4, s], rh)
        workh[...] = rh[u]
        of = sources(s)
        for o in range(REPS):
            sth[u, o] = workh[of(o)]
        rows = pl.ds(pl.multiple_of(lax.rem(me, 8) * 16, 16), 16)
        cols = pl.ds(pl.multiple_of(me // 8 * HALF, HALF), HALF)
        exchange(5, s, lambda o: sth.at[u, o], gath.at[s, rows, cols])
        for h in range(2):

            @pl.when(me // 8 == h)
            def _():
                gath[s, rows, h * HALF : (h + 1) * HALF] = sth[u, me]

    near_send(0)
    near_send(1)
    for n, (dx, dz) in enumerate([(1, 0), (0, 1), (0, 1)]):
        for device in (along(dx, dz), along(3 * dx, 3 * dz)):
            pl.semaphore_signal(hello.at[n], inc=1, device_id=device, device_id_type=MESH)
        pl.semaphore_wait(hello.at[n], 2)
    lax.fori_loop(EARLY, EARLY + 2, lambda s, _: hidden_out(s), None)
    for one in loads[hidden_loads:]:
        one.wait()

    lane = lax.broadcasted_iota(jnp.int32, (1, 128), 1)

    def project_near(s):
        slot = lax.rem(s, 2)
        x = gath[s, :, :NEAR]
        accq[slot] = jnp.dot(x, wq[:NEAR], preferred_element_type=F32)
        acck[slot] = jnp.dot(x, wkv[:NEAR], preferred_element_type=F32)

    def owned(s):
        return sources(s)(me) * STEPS + s

    def project_far(s):
        slot = lax.rem(s, 2)
        x = gath[s, :, NEAR:]
        query = accq[slot] + jnp.dot(x, wq[NEAR:], preferred_element_type=F32)
        keyval = acck[slot] + jnp.dot(x, wkv[NEAR:], preferred_element_type=F32)
        span = jnp.where(s < EARLY, me * STEPS + s, owned(s))
        angle = lens[span].astype(F32) * trig[2, :8]
        cos_p, sin_p = jnp.cos(angle)[:1], jnp.sin(angle)[:1]
        cos_t, sin_t = trig[0], trig[1]
        cosine = cos_p * cos_t - sin_p * sin_t
        sine = sin_p * cos_t + cos_p * sin_t
        sine = jnp.where(lane < HEAD_DIM // 2, -sine, sine)

        def rotate(v):
            return (v * cosine + pltpu.roll(v, HEAD_DIM // 2, 1) * sine).astype(BF)

        blocks = [rotate(query[:, h * 128 : (h + 1) * 128]) for h in range(GROUP)]
        blocks.append(rotate(keyval[:, :128]))
        blocks.append(keyval[:, 128:].astype(BF))
        return jnp.concatenate(blocks, axis=0).reshape(REPS, PIECE, 128)

    def cache_copy(s):
        return pltpu.make_async_copy(cachev.at[s], cache.at[s], out_sem.at[0, s])

    def place(s):
        rows = pl.ds(pl.multiple_of(s * SPAN_LEN + lax.rem(me, 4) * BACK, BACK), BACK)
        return back.at[rows, pl.ds(pl.multiple_of(me // 4 * 128, 128), 128)]

    def own_copy(s):
        return pltpu.make_async_copy(st4.at[s, me], place(s), out_sem.at[1, s])

    def attend(s):
        row = owned(s)
        length = lens[row]
        whole = r2[s].reshape(MSG, 128)
        fresh_k, fresh_v = whole[ROWS : ROWS + 128], whole[ROWS + 128 :]
        cachev[s, :, :128] = fresh_k
        cachev[s, :, 128:] = fresh_v
        cache_copy(s).start()
        nt = (((1,), (1,)), ((), ()))

        def page(j):
            return pool[pages[j, row]]

        position = lax.broadcasted_iota(jnp.int32, (1, 256), 1)
        t_key = lax.broadcasted_iota(jnp.int32, (BLOCK, 128), 1)
        t = lax.rem(lax.broadcasted_iota(jnp.int32, (BLOCK, 128), 0), SPAN_LEN)
        factor = SCALE * LOG2E
        for first in range(0, ROWS, BLOCK):
            q = whole[first : first + BLOCK]
            sc = lax.dot_general(q, fresh_k, nt, preferred_element_type=F32)
            sc = jnp.where(t_key <= t, sc, -jnp.inf)
            scores[:, PAGES * 128 :] = sc
            top = sc
            for j in range(0, PAGES, 2):
                keys = jnp.concatenate([page(j)[:, :128], page(j + 1)[:, :128]], axis=0)
                bias = jnp.where(position + j * 128 < length, 0.0, -jnp.inf)
                sc = lax.dot_general(q, keys, nt, preferred_element_type=F32) + bias
                scores[:, j * 128 : (j + 2) * 128] = sc
                top = jnp.maximum(top, jnp.maximum(sc[:, :128], sc[:, 128:]))
            highest = jnp.max(top, axis=1, keepdims=True) * factor
            w = jnp.exp2(scores[:, PAGES * 128 :] * factor - highest)
            total = w
            summed = jnp.dot(w.astype(BF), fresh_v, preferred_element_type=F32)
            for j in range(0, PAGES, 2):
                values = jnp.concatenate([page(j)[:, 128:], page(j + 1)[:, 128:]], axis=0)
                w = jnp.exp2(scores[:, j * 128 : (j + 2) * 128] * factor - highest)
                total = total + (w[:, :128] + w[:, 128:])
                summed = summed + jnp.dot(w.astype(BF), values, preferred_element_type=F32)
            total = jnp.sum(total, axis=1, keepdims=True)
            done = (summed / total).astype(BF).reshape(BLOCK // BACK, BACK, 128)
            om[s, first // BACK : (first + BLOCK) // BACK] = done

    def between(s, low, high):
        return pl.when((s >= low) & (s < high))

    def late_and_early(late, early, run):
        def one(n, carry):
            s = jnp.where(n == 0, late, early)

            @between(s, jnp.where(n == 0, EARLY, 0), jnp.where(n == 0, STEPS, EARLY))
            def _():
                run(s)

            return carry

        lax.fori_loop(0, 2, one, 0)

    def back_on(s):
        arrived(x_recv.at[2, s], r3)
        work3[...] = r3[s]
        for r in range(REPS):
            st4[s, r] = work3[owner[r * STEPS + s]]
        exchange(3, s, lambda r: st4.at[s, r], place(s))
        own_copy(s).start()

    def settle(s):
        for kind in range(8):
            y_copy(kind, s).wait_send()
        cache_copy(s).wait()
        arrived(x_send.at[2, s], om)

        @pl.when(s < EARLY)
        def _():
            arrived(x_send.at[0, s], msg)
            arrived(x_send.at[1, s], st2)

        @pl.when(s >= EARLY)
        def _():
            arrived(x_send.at[4, s], rh)
            arrived(x_send.at[5, s], sth)

    def finish(s):
        own_copy(s).wait()
        arrived(x_send.at[3, s], st4)
        arrived(x_recv.at[3, s], st4)

    def work(s):
        @pl.when(s < EARLY)
        def _():
            arrived(x_recv.at[1, s], r1)

        attend(s)
        exchange(2, s, lambda j: om.at[s, j], r3.at[s, me])
        r3[s, me] = om[s, me]

    def far_on(s):
        y_copy(3, s).wait_recv()
        y_copy(4, s).wait_recv()
        y_copy(7, s).start()

    def step(it, carry):
        @between(it, 0, STEPS)
        def _():
            y_copy(0, it).wait_recv()
            y_copy(3, it).start()
            y_copy(5, it).start()
            y_copy(1, it).wait_recv()
            y_copy(4, it).start()
            y_copy(6, it).start()

        @between(it - 1, 0, STEPS - 1)
        def _():
            far_on(it - 1)

        @between(it + 3, EARLY, STEPS)
        def _():
            hidden_on(it + 3)

        @between(it + 5, EARLY + 2, STEPS)
        def _():
            hidden_out(it + 5)

        @between(it, 0, STEPS)
        def _():
            for kind in (2, 5, 6):
                y_copy(kind, it).wait_recv()
            project_near(it)

        @between(it + 2, 2, STEPS)
        def _():
            @pl.when(it + 2 >= EARLY)
            def _():
                arrived(x_recv.at[5, it + 2], rh)

            near_send(it + 2)

        @between(it - 1, 0, STEPS)
        def _():
            s = it - 1
            y_copy(7, s).wait_recv()
            whole = project_far(s)

            @pl.when(s < EARLY)
            def _():
                msg[s] = whole
                exchange(0, s, lambda j: msg.at[s, j], r1.at[s, me])
                r1[s, me] = msg[s, me]

            @pl.when(s >= EARLY)
            def _():
                r2[s] = whole

        @pl.when(it == STEPS - 1)
        def _():
            far_on(it)

        late_and_early(it - 1, it - 3, work)
        late_and_early(it - 2, it - 4, back_on)

        @between(it - 2, 0, EARLY)
        def _():
            s = it - 2
            arrived(x_recv.at[0, s], r1)
            work1[...] = r1[s]
            of = sources(s)
            for o in range(REPS):
                st2[s, o] = work1[of(o)]
            exchange(1, s, lambda o: st2.at[s, o], r2.at[s, me])
            r2[s, me] = st2[s, me]

        late_and_early(it - 2, it - 5, settle)
        late_and_early(it - 3, it - 6, finish)
        return carry

    lax.fori_loop(0, STEPS + 3, step, 0)


def hand_over(back, fresh, out, cache, out_held, cache_held, sem):
    parts = []
    for s in range(0, STEPS, 2):
        rows = pl.ds(s * SPAN_LEN, 2 * SPAN_LEN)
        parts.append((back.at[rows], out_held.at[rows], out.at[rows]))
    for s in range(0, STEPS, 4):
        spans = pl.ds(s, 4)
        parts.append((fresh.at[spans], cache_held.at[spans], cache.at[spans]))
    first = [pltpu.make_async_copy(p[0], p[1], sem.at[0, i]) for i, p in enumerate(parts)]
    second = [pltpu.make_async_copy(p[1], p[2], sem.at[1, i]) for i, p in enumerate(parts)]
    for copy in first:
        copy.start()
    for one, two in zip(first, second):
        one.wait()
        two.start()
    for copy in second:
        copy.wait()


def trig_tables():
    i = np.arange(64, dtype=np.float64)
    frequency = np.concatenate([ROPE_BASE ** (-2.0 * i / HEAD_DIM)] * 2)
    angle = np.arange(SPAN_LEN, dtype=np.float64)[:, None] * frequency[None, :]
    wide = np.broadcast_to(frequency[None, :], (SPAN_LEN, HEAD_DIM))
    return np.stack([np.cos(angle), np.sin(angle), wide]).astype(np.float32)


def body(hidden, w_query, w_keyval, kv_pool, prefix_len, owner, block_table):
    v = pltpu.VMEM
    dma = pltpu.SemaphoreType.DMA
    any_spec = pl.BlockSpec(memory_space=pl.ANY)
    vmem = pl.BlockSpec(memory_space=pltpu.VMEM)
    shapes = (
        jax.ShapeDtypeStruct((STEPS * SPAN_LEN, GROUP * 128), BF),
        jax.ShapeDtypeStruct((STEPS, SPAN_LEN, 256), BF),
    )
    results = pl.pallas_call(
        kernel,
        out_shape=shapes,
        in_specs=[pl.BlockSpec(memory_space=pltpu.SMEM)] * 3 + [any_spec] * 4 + [vmem],
        out_specs=(any_spec, any_spec),
        scratch_shapes=[
            v((STEPS, SPAN_LEN, 8 * CHUNK), BF),
            v((8 * CHUNK, GROUP * 128), BF),
            v((8 * CHUNK, 256), BF),
            v((128, 128, 256), BF),
            v((2, SPAN_LEN, GROUP * 128), F32),
            v((2, SPAN_LEN, 256), F32),
            v((LATE, 2, SPAN_LEN, HALF), BF),
            v((LATE, REPS, 16, HALF), BF),
            v((LATE, REPS, 16, HALF), BF),
            v((EARLY, REPS, PIECE, 128), BF),
            v((EARLY, REPS, PIECE, 128), BF),
            v((EARLY, REPS, PIECE, 128), BF),
            v((STEPS, REPS, PIECE, 128), BF),
            v((STEPS, REPS, BACK, 128), BF),
            v((STEPS, REPS, BACK, 128), BF),
            v((STEPS, REPS, BACK, 128), BF),
            v((BLOCK, KEYS), F32),
            v((REPS, 16, HALF), BF),
            v((REPS, PIECE, 128), BF),
            v((REPS, BACK, 128), BF),
            v((STEPS, SPAN_LEN, 256), BF),
            dma((EARLY + 2 * LATE + 17,)),
            dma((2, STEPS)),
            pltpu.SemaphoreType.REGULAR((3,)),
            dma((8, STEPS)),
            dma((8, STEPS)),
            dma((6, STEPS)),
            dma((6, STEPS)),
        ],
        compiler_params=pltpu.CompilerParams(
            collective_id=0, has_side_effects=True, vmem_limit_bytes=62 * 1024 * 1024
        ),
        cost_estimate=pl.CostEstimate(
            flops=18_000_000_000, bytes_accessed=24_000_000, transcendentals=9_000_000
        ),
    )(prefix_len, owner, block_table.T, hidden, w_query, w_keyval, kv_pool, jnp.asarray(trig_tables()))
    return pl.pallas_call(
        hand_over,
        out_shape=shapes,
        in_specs=[any_spec] * 2,
        out_specs=(any_spec, any_spec),
        scratch_shapes=[v(shapes[0].shape, BF), v(shapes[1].shape, BF), dma((2, STEPS))],
    )(*results)


def solution(mesh):
    placed = (P("rep", "tp"), P(None, "tp"), P(None, "tp"), P("rep", None, "tp"), P(), P(), P())
    return jax.shard_map(
        body,
        mesh=mesh,
        in_specs=placed,
        out_specs=(P("rep", "tp"), P("rep", None, "tp")),
        check_vma=False,
    )
```

```python
import math

import jax
import jax.numpy as jnp
import numpy as np
from jax import lax
from jax.experimental import pallas as pl
from jax.experimental.pallas import tpu as pltpu
from jax.sharding import PartitionSpec as P

HEAD_DIM = 128
SPAN_LEN = 128
ROPE_BASE = 500000.0
MESH = pl.DeviceIdType.MESH
BF = jnp.bfloat16
F32 = jnp.float32

REPS = 16
STEPS = 8
PAGES = 16
GROUP = 4
ROWS = GROUP * SPAN_LEN
MSG = ROWS + 2 * SPAN_LEN
PIECE = MSG // REPS
BACK = ROWS // REPS
KEYS = PAGES * 128 + SPAN_LEN
CHUNK = 1024
NEAR = 6 * CHUNK
SCALE = 1.0 / math.sqrt(HEAD_DIM)
LOG2E = math.log2(math.e)

EARLY = 3
LATE = STEPS - EARLY
HALF = CHUNK // 2
BLOCK = 256
OFFSETS = [
    (2, 2), (2, 1), (1, 2), (2, 3), (3, 2), (1, 1), (3, 3), (1, 3), (3, 1),
    (0, 2), (2, 0), (0, 1), (1, 0), (0, 3), (3, 0),
]


def kernel(
    lens, owner, pages, hid, wq_h, wkv_h, pool_h, trig, back, cache,
    gath, wq, wkv, pool, accq, acck, hv, rh, sth, msg, r1, st2, r2, om, r3, st4,
    scores, workh, work1, work3, cachev,
    local_sem, out_sem, hello, y_send, y_recv, x_send, x_recv,
):
    me = lax.axis_index("rep")
    tp = lax.axis_index("tp")
    y, c = tp // 2, lax.rem(tp, 2)
    up = (me, lax.rem(y + 1, 4) * 2 + c)
    down = (me, lax.rem(y + 3, 4) * 2 + c)
    sib = (me, y * 2 + 1 - c)
    peers = [
        lax.rem(me // 4 + dx, 4) * 4 + lax.rem(lax.rem(me, 4) + dz, 4) for dx, dz in OFFSETS
    ]

    loads = []

    def load(src, dst):
        loads.append(pltpu.make_async_copy(src, dst, local_sem.at[len(loads)]))

    for s in range(EARLY):
        load(hid.at[pl.ds(s * SPAN_LEN, SPAN_LEN)], gath.at[s, :, pl.ds(0, CHUNK)])
    for s in range(LATE):
        for h in range(2):
            load(
                hid.at[pl.ds((EARLY + s) * SPAN_LEN, SPAN_LEN), pl.ds(h * HALF, HALF)],
                hv.at[s, h],
            )
    hidden_loads = len(loads)
    for slot, (rel, other) in enumerate(
        [(0, 0), (0, 1), (3, 0), (1, 0), (3, 1), (1, 1), (2, 0), (2, 1)]
    ):
        core = c if other == 0 else 1 - c
        rows = pl.ds(pl.multiple_of((lax.rem(y + rel, 4) * 2 + core) * CHUNK, CHUNK), CHUNK)
        place = pl.ds(slot * CHUNK, CHUNK)
        load(wq_h.at[rows], wq.at[place])
        load(wkv_h.at[rows], wkv.at[place])
    load(pool_h, pool)
    for one in loads:
        one.start()

    def along(dx, dz):
        return (lax.rem(me // 4 + dx, 4) * 4 + lax.rem(lax.rem(me, 4) + dz, 4), tp)

    barrier = pltpu.get_barrier_semaphore()
    for device in (up, down, sib, along(1, 0), along(3, 0), along(0, 1), along(0, 3)):
        pl.semaphore_signal(barrier, inc=1, device_id=device, device_id_type=MESH)
    for one in loads[:hidden_loads]:
        one.wait()
    pl.semaphore_wait(barrier, 7)

    def remote(src, dst, send, recv, device):
        return pltpu.make_async_remote_copy(
            src_ref=src, dst_ref=dst, send_sem=send, recv_sem=recv,
            device_id=device, device_id_type=MESH,
        )

    def part(s, slot, first=0, count=SPAN_LEN):
        return gath.at[s, pl.ds(first, count), pl.ds(slot * CHUNK, CHUNK)]

    half = SPAN_LEN // 2

    def y_copy(kind, s):
        sems = (y_send.at[kind, s], y_recv.at[kind, s])
        if kind == 0:
            return remote(part(s, 0), part(s, 2), *sems, up)
        if kind == 1:
            return remote(part(s, 0), part(s, 3), *sems, down)
        if kind == 2:
            return remote(part(s, 0), part(s, 1), *sems, sib)
        if kind == 3:
            return remote(part(s, 2, 0, half), part(s, 6, 0, half), *sems, up)
        if kind == 4:
            return remote(part(s, 3, half, half), part(s, 6, half, half), *sems, down)
        if kind == 5:
            return remote(part(s, 2), part(s, 4), *sems, sib)
        if kind == 6:
            return remote(part(s, 3), part(s, 5), *sems, sib)
        return remote(part(s, 6), part(s, 7), *sems, sib)

    def near_send(s):
        for kind in (0, 1, 2):
            y_copy(kind, s).start()

    def exchange(phase, s, src, dst):
        for peer in peers:
            remote(
                src(peer), dst, x_send.at[phase, s], x_recv.at[phase, s], (peer, tp)
            ).start()

    def arrived(sem, ref):
        ref = ref.at[0, pl.ds(0, REPS - 1)]
        pltpu.make_async_copy(ref, ref, sem).wait()

    def sources(s):
        owners = [owner[r * STEPS + s] for r in range(REPS)]

        def of(o):
            found = jnp.int32(0)
            for r in range(1, REPS):
                found = jnp.where(owners[r] == o, r, found)
            return found

        return of

    def hidden_out(s):
        u = s - EARLY

        def src(j):
            return hv.at[u, j // 8, pl.ds(pl.multiple_of(lax.rem(j, 8) * 16, 16), 16)]

        exchange(4, s, src, rh.at[u, me])
        rh[u, me] = hv[u, me // 8, pl.ds(pl.multiple_of(lax.rem(me, 8) * 16, 16), 16)]

    def hidden_on(s):
        u = s - EARLY
        arrived(x_recv.at[4, s], rh)
        workh[...] = rh[u]
        of = sources(s)
        for o in range(REPS):
            sth[u, o] = workh[of(o)]
        rows = pl.ds(pl.multiple_of(lax.rem(me, 8) * 16, 16), 16)
        cols = pl.ds(pl.multiple_of(me // 8 * HALF, HALF), HALF)
        exchange(5, s, lambda o: sth.at[u, o], gath.at[s, rows, cols])
        for h in range(2):

            @pl.when(me // 8 == h)
            def _():
                gath[s, rows, h * HALF : (h + 1) * HALF] = sth[u, me]

    near_send(0)
    near_send(1)
    for n, (dx, dz) in enumerate([(1, 0), (0, 1), (0, 1)]):
        for device in (along(dx, dz), along(3 * dx, 3 * dz)):
            pl.semaphore_signal(hello.at[n], inc=1, device_id=device, device_id_type=MESH)
        pl.semaphore_wait(hello.at[n], 2)
    lax.fori_loop(EARLY, EARLY + 2, lambda s, _: hidden_out(s), None)
    for one in loads[hidden_loads:]:
        one.wait()

    lane = lax.broadcasted_iota(jnp.int32, (1, 128), 1)

    def project_near(s):
        slot = lax.rem(s, 2)
        x = gath[s, :, :NEAR]
        accq[slot] = jnp.dot(x, wq[:NEAR], preferred_element_type=F32)
        acck[slot] = jnp.dot(x, wkv[:NEAR], preferred_element_type=F32)

    def owned(s):
        return sources(s)(me) * STEPS + s

    def project_far(s):
        slot = lax.rem(s, 2)
        x = gath[s, :, NEAR:]
        query = accq[slot] + jnp.dot(x, wq[NEAR:], preferred_element_type=F32)
        keyval = acck[slot] + jnp.dot(x, wkv[NEAR:], preferred_element_type=F32)
        span = jnp.where(s < EARLY, me * STEPS + s, owned(s))
        angle = lens[span].astype(F32) * trig[2, :8]
        cos_p, sin_p = jnp.cos(angle)[:1], jnp.sin(angle)[:1]
        cos_t, sin_t = trig[0], trig[1]
        cosine = cos_p * cos_t - sin_p * sin_t
        sine = sin_p * cos_t + cos_p * sin_t
        sine = jnp.where(lane < HEAD_DIM // 2, -sine, sine)

        def rotate(v):
            return (v * cosine + pltpu.roll(v, HEAD_DIM // 2, 1) * sine).astype(BF)

        blocks = [rotate(query[:, h * 128 : (h + 1) * 128]) for h in range(GROUP)]
        blocks.append(rotate(keyval[:, :128]))
        blocks.append(keyval[:, 128:].astype(BF))
        return jnp.concatenate(blocks, axis=0).reshape(REPS, PIECE, 128)

    def cache_copy(s):
        return pltpu.make_async_copy(cachev.at[s], cache.at[s], out_sem.at[0, s])

    def place(s):
        rows = pl.ds(pl.multiple_of(s * SPAN_LEN + lax.rem(me, 4) * BACK, BACK), BACK)
        return back.at[rows, pl.ds(pl.multiple_of(me // 4 * 128, 128), 128)]

    def own_copy(s):
        return pltpu.make_async_copy(st4.at[s, me], place(s), out_sem.at[1, s])

    def attend(s):
        row = owned(s)
        length = lens[row]
        whole = r2[s].reshape(MSG, 128)
        fresh_k, fresh_v = whole[ROWS : ROWS + 128], whole[ROWS + 128 :]
        cachev[s, :, :128] = fresh_k
        cachev[s, :, 128:] = fresh_v
        cache_copy(s).start()
        nt = (((1,), (1,)), ((), ()))

        def page(j):
            return pool[pages[j, row]]

        position = lax.broadcasted_iota(jnp.int32, (1, 256), 1)
        t_key = lax.broadcasted_iota(jnp.int32, (BLOCK, 128), 1)
        t = lax.rem(lax.broadcasted_iota(jnp.int32, (BLOCK, 128), 0), SPAN_LEN)
        factor = SCALE * LOG2E
        for first in range(0, ROWS, BLOCK):
            q = whole[first : first + BLOCK]
            sc = lax.dot_general(q, fresh_k, nt, preferred_element_type=F32)
            sc = jnp.where(t_key <= t, sc, -jnp.inf)
            scores[:, PAGES * 128 :] = sc
            top = sc
            for j in range(0, PAGES, 2):
                keys = jnp.concatenate([page(j)[:, :128], page(j + 1)[:, :128]], axis=0)
                bias = jnp.where(position + j * 128 < length, 0.0, -jnp.inf)
                sc = lax.dot_general(q, keys, nt, preferred_element_type=F32) + bias
                scores[:, j * 128 : (j + 2) * 128] = sc
                top = jnp.maximum(top, jnp.maximum(sc[:, :128], sc[:, 128:]))
            highest = jnp.max(top, axis=1, keepdims=True) * factor
            w = jnp.exp2(scores[:, PAGES * 128 :] * factor - highest)
            total = w
            summed = jnp.dot(w.astype(BF), fresh_v, preferred_element_type=F32)
            for j in range(0, PAGES, 2):
                values = jnp.concatenate([page(j)[:, 128:], page(j + 1)[:, 128:]], axis=0)
                w = jnp.exp2(scores[:, j * 128 : (j + 2) * 128] * factor - highest)
                total = total + (w[:, :128] + w[:, 128:])
                summed = summed + jnp.dot(w.astype(BF), values, preferred_element_type=F32)
            total = jnp.sum(total, axis=1, keepdims=True)
            done = (summed / total).astype(BF).reshape(BLOCK // BACK, BACK, 128)
            om[s, first // BACK : (first + BLOCK) // BACK] = done

    def between(s, low, high):
        return pl.when((s >= low) & (s < high))

    def late_and_early(late, early, run):
        def one(n, carry):
            s = jnp.where(n == 0, late, early)

            @between(s, jnp.where(n == 0, EARLY, 0), jnp.where(n == 0, STEPS, EARLY))
            def _():
                run(s)

            return carry

        lax.fori_loop(0, 2, one, 0)

    def back_on(s):
        arrived(x_recv.at[2, s], r3)
        work3[...] = r3[s]
        for r in range(REPS):
            st4[s, r] = work3[owner[r * STEPS + s]]
        exchange(3, s, lambda r: st4.at[s, r], place(s))
        own_copy(s).start()

    def settle(s):
        for kind in range(8):
            y_copy(kind, s).wait_send()
        cache_copy(s).wait()
        arrived(x_send.at[2, s], om)

        @pl.when(s < EARLY)
        def _():
            arrived(x_send.at[0, s], msg)
            arrived(x_send.at[1, s], st2)

        @pl.when(s >= EARLY)
        def _():
            arrived(x_send.at[4, s], rh)
            arrived(x_send.at[5, s], sth)

    def finish(s):
        own_copy(s).wait()
        arrived(x_send.at[3, s], st4)
        arrived(x_recv.at[3, s], st4)

    def work(s):
        @pl.when(s < EARLY)
        def _():
            arrived(x_recv.at[1, s], r1)

        attend(s)
        exchange(2, s, lambda j: om.at[s, j], r3.at[s, me])
        r3[s, me] = om[s, me]

    def far_on(s):
        y_copy(3, s).wait_recv()
        y_copy(4, s).wait_recv()
        y_copy(7, s).start()

    def follow(it, carry):
        late_and_early(it - 2, it - 4, back_on)

        @between(it - 2, 0, EARLY)
        def _():
            s = it - 2
            arrived(x_recv.at[0, s], r1)
            work1[...] = r1[s]
            of = sources(s)
            for o in range(REPS):
                st2[s, o] = work1[of(o)]
            exchange(1, s, lambda o: st2.at[s, o], r2.at[s, me])
            r2[s, me] = st2[s, me]

        late_and_early(it - 2, it - 5, settle)
        late_and_early(it - 4, it - 7, finish)
        return carry

    def step(it, carry):
        @between(it, 0, STEPS)
        def _():
            y_copy(0, it).wait_recv()
            y_copy(3, it).start()
            y_copy(5, it).start()
            y_copy(1, it).wait_recv()
            y_copy(4, it).start()
            y_copy(6, it).start()

        @between(it - 1, 0, STEPS - 1)
        def _():
            far_on(it - 1)

        @between(it + 3, EARLY, STEPS)
        def _():
            hidden_on(it + 3)

        @between(it + 5, EARLY + 2, STEPS)
        def _():
            hidden_out(it + 5)

        @between(it, 0, STEPS)
        def _():
            for kind in (2, 5, 6):
                y_copy(kind, it).wait_recv()
            project_near(it)

        @between(it + 2, 2, STEPS)
        def _():
            @pl.when(it + 2 >= EARLY)
            def _():
                arrived(x_recv.at[5, it + 2], rh)

            near_send(it + 2)

        @between(it - 1, 0, STEPS)
        def _():
            s = it - 1
            y_copy(7, s).wait_recv()
            whole = project_far(s)

            @pl.when(s < EARLY)
            def _():
                msg[s] = whole
                exchange(0, s, lambda j: msg.at[s, j], r1.at[s, me])
                r1[s, me] = msg[s, me]

            @pl.when(s >= EARLY)
            def _():
                r2[s] = whole

        @pl.when(it == STEPS - 1)
        def _():
            far_on(it)

        late_and_early(it - 1, it - 3, work)
        last = STEPS - 1
        lax.fori_loop(
            jnp.where(it == last + 1, last, it), jnp.where(it == last, it, it + 1), follow, 0
        )
        return carry

    lax.fori_loop(0, STEPS + 4, step, 0)


def hand_over(back, fresh, out, cache, out_held, cache_held, sem):
    parts = []
    for s in range(0, STEPS, 2):
        rows = pl.ds(s * SPAN_LEN, 2 * SPAN_LEN)
        parts.append((back.at[rows], out_held.at[rows], out.at[rows]))
    for s in range(0, STEPS, 4):
        spans = pl.ds(s, 4)
        parts.append((fresh.at[spans], cache_held.at[spans], cache.at[spans]))
    first = [pltpu.make_async_copy(p[0], p[1], sem.at[0, i]) for i, p in enumerate(parts)]
    second = [pltpu.make_async_copy(p[1], p[2], sem.at[1, i]) for i, p in enumerate(parts)]
    for copy in first:
        copy.start()
    for one, two in zip(first, second):
        one.wait()
        two.start()
    for copy in second:
        copy.wait()


def trig_tables():
    i = np.arange(64, dtype=np.float64)
    frequency = np.concatenate([ROPE_BASE ** (-2.0 * i / HEAD_DIM)] * 2)
    angle = np.arange(SPAN_LEN, dtype=np.float64)[:, None] * frequency[None, :]
    wide = np.broadcast_to(frequency[None, :], (SPAN_LEN, HEAD_DIM))
    return np.stack([np.cos(angle), np.sin(angle), wide]).astype(np.float32)


def body(hidden, w_query, w_keyval, kv_pool, prefix_len, owner, block_table):
    v = pltpu.VMEM
    dma = pltpu.SemaphoreType.DMA
    any_spec = pl.BlockSpec(memory_space=pl.ANY)
    vmem = pl.BlockSpec(memory_space=pltpu.VMEM)
    shapes = (
        jax.ShapeDtypeStruct((STEPS * SPAN_LEN, GROUP * 128), BF),
        jax.ShapeDtypeStruct((STEPS, SPAN_LEN, 256), BF),
    )
    results = pl.pallas_call(
        kernel,
        out_shape=shapes,
        in_specs=[pl.BlockSpec(memory_space=pltpu.SMEM)] * 3 + [any_spec] * 4 + [vmem],
        out_specs=(any_spec, any_spec),
        scratch_shapes=[
            v((STEPS, SPAN_LEN, 8 * CHUNK), BF),
            v((8 * CHUNK, GROUP * 128), BF),
            v((8 * CHUNK, 256), BF),
            v((128, 128, 256), BF),
            v((2, SPAN_LEN, GROUP * 128), F32),
            v((2, SPAN_LEN, 256), F32),
            v((LATE, 2, SPAN_LEN, HALF), BF),
            v((LATE, REPS, 16, HALF), BF),
            v((LATE, REPS, 16, HALF), BF),
            v((EARLY, REPS, PIECE, 128), BF),
            v((EARLY, REPS, PIECE, 128), BF),
            v((EARLY, REPS, PIECE, 128), BF),
            v((STEPS, REPS, PIECE, 128), BF),
            v((STEPS, REPS, BACK, 128), BF),
            v((STEPS, REPS, BACK, 128), BF),
            v((STEPS, REPS, BACK, 128), BF),
            v((BLOCK, KEYS), F32),
            v((REPS, 16, HALF), BF),
            v((REPS, PIECE, 128), BF),
            v((REPS, BACK, 128), BF),
            v((STEPS, SPAN_LEN, 256), BF),
            dma((EARLY + 2 * LATE + 17,)),
            dma((2, STEPS)),
            pltpu.SemaphoreType.REGULAR((3,)),
            dma((8, STEPS)),
            dma((8, STEPS)),
            dma((6, STEPS)),
            dma((6, STEPS)),
        ],
        compiler_params=pltpu.CompilerParams(
            collective_id=0, has_side_effects=True, vmem_limit_bytes=62 * 1024 * 1024
        ),
        cost_estimate=pl.CostEstimate(
            flops=18_000_000_000, bytes_accessed=24_000_000, transcendentals=9_000_000
        ),
    )(prefix_len, owner, block_table.T, hidden, w_query, w_keyval, kv_pool, jnp.asarray(trig_tables()))
    return pl.pallas_call(
        hand_over,
        out_shape=shapes,
        in_specs=[any_spec] * 2,
        out_specs=(any_spec, any_spec),
        scratch_shapes=[v(shapes[0].shape, BF), v(shapes[1].shape, BF), dma((2, STEPS))],
    )(*results)


def solution(mesh):
    placed = (P("rep", "tp"), P(None, "tp"), P(None, "tp"), P("rep", None, "tp"), P(), P(), P())
    return jax.shard_map(
        body,
        mesh=mesh,
        in_specs=placed,
        out_specs=(P("rep", "tp"), P("rep", None, "tp")),
        check_vma=False,
    )
```

```python
import math

import jax
import jax.numpy as jnp
import numpy as np
from jax import lax
from jax.experimental import pallas as pl
from jax.experimental.pallas import tpu as pltpu
from jax.sharding import PartitionSpec as P

HEAD_DIM = 128
SPAN_LEN = 128
ROPE_BASE = 500000.0
MESH = pl.DeviceIdType.MESH
BF = jnp.bfloat16
F32 = jnp.float32

REPS = 16
STEPS = 8
PAGES = 16
GROUP = 4
ROWS = GROUP * SPAN_LEN
MSG = ROWS + 2 * SPAN_LEN
PIECE = MSG // REPS
BACK = ROWS // REPS
KEYS = PAGES * 128 + SPAN_LEN
CHUNK = 1024
NEAR = 6 * CHUNK
SCALE = 1.0 / math.sqrt(HEAD_DIM)
LOG2E = math.log2(math.e)

EARLY = 3
LATE = STEPS - EARLY
HALF = CHUNK // 2
BLOCK = 256
OFFSETS = [
    (2, 2), (2, 1), (1, 2), (2, 3), (3, 2), (1, 1), (3, 3), (1, 3), (3, 1),
    (0, 2), (2, 0), (0, 1), (1, 0), (0, 3), (3, 0),
]


def kernel(
    lens, owner, pages, hid, wq_h, wkv_h, pool_h, trig, back, cache,
    gath, wq, wkv, pool, accq, acck, hv, rh, sth, msg, r1, st2, r2, om, r3, st4,
    scores, workh, work1, work3, cachev,
    local_sem, out_sem, hello, y_send, y_recv, x_send, x_recv,
):
    me = lax.axis_index("rep")
    tp = lax.axis_index("tp")
    y, c = tp // 2, lax.rem(tp, 2)
    up = (me, lax.rem(y + 1, 4) * 2 + c)
    down = (me, lax.rem(y + 3, 4) * 2 + c)
    sib = (me, y * 2 + 1 - c)
    peers = [
        lax.rem(me // 4 + dx, 4) * 4 + lax.rem(lax.rem(me, 4) + dz, 4) for dx, dz in OFFSETS
    ]

    loads = []

    def load(src, dst):
        loads.append(pltpu.make_async_copy(src, dst, local_sem.at[len(loads)]))

    for s in range(EARLY):
        load(hid.at[pl.ds(s * SPAN_LEN, SPAN_LEN)], gath.at[s, :, pl.ds(0, CHUNK)])
    for s in range(LATE):
        for h in range(2):
            load(
                hid.at[pl.ds((EARLY + s) * SPAN_LEN, SPAN_LEN), pl.ds(h * HALF, HALF)],
                hv.at[s, h],
            )
    hidden_loads = len(loads)
    for slot, (rel, other) in enumerate(
        [(0, 0), (0, 1), (3, 0), (1, 0), (3, 1), (1, 1), (2, 0), (2, 1)]
    ):
        core = c if other == 0 else 1 - c
        rows = pl.ds(pl.multiple_of((lax.rem(y + rel, 4) * 2 + core) * CHUNK, CHUNK), CHUNK)
        place = pl.ds(slot * CHUNK, CHUNK)
        load(wq_h.at[rows], wq.at[place])
        load(wkv_h.at[rows], wkv.at[place])
    load(pool_h, pool)
    for one in loads:
        one.start()

    def along(dx, dz):
        return (lax.rem(me // 4 + dx, 4) * 4 + lax.rem(lax.rem(me, 4) + dz, 4), tp)

    barrier = pltpu.get_barrier_semaphore()
    for device in (up, down, sib, along(1, 0), along(3, 0), along(0, 1), along(0, 3)):
        pl.semaphore_signal(barrier, inc=1, device_id=device, device_id_type=MESH)
    for one in loads[:hidden_loads]:
        one.wait()
    pl.semaphore_wait(barrier, 7)

    def remote(src, dst, send, recv, device):
        return pltpu.make_async_remote_copy(
            src_ref=src, dst_ref=dst, send_sem=send, recv_sem=recv,
            device_id=device, device_id_type=MESH,
        )

    def part(s, slot, first=0, count=SPAN_LEN):
        return gath.at[s, pl.ds(first, count), pl.ds(slot * CHUNK, CHUNK)]

    half = SPAN_LEN // 2

    def y_copy(kind, s):
        sems = (y_send.at[kind, s], y_recv.at[kind, s])
        if kind == 0:
            return remote(part(s, 0), part(s, 2), *sems, up)
        if kind == 1:
            return remote(part(s, 0), part(s, 3), *sems, down)
        if kind == 2:
            return remote(part(s, 0), part(s, 1), *sems, sib)
        if kind == 3:
            return remote(part(s, 2, 0, half), part(s, 6, 0, half), *sems, up)
        if kind == 4:
            return remote(part(s, 3, half, half), part(s, 6, half, half), *sems, down)
        if kind == 5:
            return remote(part(s, 2), part(s, 4), *sems, sib)
        if kind == 6:
            return remote(part(s, 3), part(s, 5), *sems, sib)
        return remote(part(s, 6), part(s, 7), *sems, sib)

    def near_send(s):
        for kind in (0, 1, 2):
            y_copy(kind, s).start()

    def exchange(phase, s, src, dst):
        for peer in peers:
            remote(
                src(peer), dst, x_send.at[phase, s], x_recv.at[phase, s], (peer, tp)
            ).start()

    def arrived(sem, ref):
        ref = ref.at[0, pl.ds(0, REPS - 1)]
        pltpu.make_async_copy(ref, ref, sem).wait()

    def sources(s):
        owners = [owner[r * STEPS + s] for r in range(REPS)]

        def of(o):
            found = jnp.int32(0)
            for r in range(1, REPS):
                found = jnp.where(owners[r] == o, r, found)
            return found

        return of

    def hidden_out(s):
        u = s - EARLY

        def src(j):
            return hv.at[u, j // 8, pl.ds(pl.multiple_of(lax.rem(j, 8) * 16, 16), 16)]

        exchange(4, s, src, rh.at[u, me])
        rh[u, me] = hv[u, me // 8, pl.ds(pl.multiple_of(lax.rem(me, 8) * 16, 16), 16)]

    def hidden_on(s):
        u = s - EARLY
        arrived(x_recv.at[4, s], rh)
        workh[...] = rh[u]
        of = sources(s)
        for o in range(REPS):
            sth[u, o] = workh[of(o)]
        rows = pl.ds(pl.multiple_of(lax.rem(me, 8) * 16, 16), 16)
        cols = pl.ds(pl.multiple_of(me // 8 * HALF, HALF), HALF)
        exchange(5, s, lambda o: sth.at[u, o], gath.at[s, rows, cols])
        for h in range(2):

            @pl.when(me // 8 == h)
            def _():
                gath[s, rows, h * HALF : (h + 1) * HALF] = sth[u, me]

    near_send(0)
    near_send(1)
    for n, (dx, dz) in enumerate([(1, 0), (0, 1), (0, 1)]):
        for device in (along(dx, dz), along(3 * dx, 3 * dz)):
            pl.semaphore_signal(hello.at[n], inc=1, device_id=device, device_id_type=MESH)
        pl.semaphore_wait(hello.at[n], 2)
    lax.fori_loop(EARLY, EARLY + 2, lambda s, _: hidden_out(s), None)
    for one in loads[hidden_loads:]:
        one.wait()

    lane = lax.broadcasted_iota(jnp.int32, (1, 128), 1)

    def project_near(s):
        slot = lax.rem(s, 2)
        x = gath[s, :, :NEAR]
        accq[slot] = jnp.dot(x, wq[:NEAR], preferred_element_type=F32)
        acck[slot] = jnp.dot(x, wkv[:NEAR], preferred_element_type=F32)

    def owned(s):
        return sources(s)(me) * STEPS + s

    def project_far(s):
        slot = lax.rem(s, 2)
        x = gath[s, :, NEAR:]
        query = accq[slot] + jnp.dot(x, wq[NEAR:], preferred_element_type=F32)
        keyval = acck[slot] + jnp.dot(x, wkv[NEAR:], preferred_element_type=F32)
        span = jnp.where(s < EARLY, me * STEPS + s, owned(s))
        angle = lens[span].astype(F32) * trig[2, :8]
        cos_p, sin_p = jnp.cos(angle)[:1], jnp.sin(angle)[:1]
        cos_t, sin_t = trig[0], trig[1]
        cosine = cos_p * cos_t - sin_p * sin_t
        sine = sin_p * cos_t + cos_p * sin_t
        sine = jnp.where(lane < HEAD_DIM // 2, -sine, sine)

        def rotate(v):
            return (v * cosine + pltpu.roll(v, HEAD_DIM // 2, 1) * sine).astype(BF)

        blocks = [rotate(query[:, h * 128 : (h + 1) * 128]) for h in range(GROUP)]
        blocks.append(rotate(keyval[:, :128]))
        blocks.append(keyval[:, 128:].astype(BF))
        return jnp.concatenate(blocks, axis=0).reshape(REPS, PIECE, 128)

    def cache_copy(s):
        return pltpu.make_async_copy(cachev.at[s], cache.at[s], out_sem.at[0, s])

    def place(s):
        rows = pl.ds(pl.multiple_of(s * SPAN_LEN + lax.rem(me, 4) * BACK, BACK), BACK)
        return back.at[rows, pl.ds(pl.multiple_of(me // 4 * 128, 128), 128)]

    def own_copy(s):
        return pltpu.make_async_copy(st4.at[s, me], place(s), out_sem.at[1, s])

    def result_out(s, begin):
        count = BLOCK // BACK
        for d in (6, 5, 7, 2, 3, 1, 4, 0):
            j = begin + lax.rem(lax.rem(me, count) + d, count)

            def send(j=j):
                remote(
                    om.at[s, j], r3.at[s, me], x_send.at[2, s], x_recv.at[2, s], (j, tp)
                ).start()

            if d:
                send()
            else:
                pl.when(j != me)(send)

    def attend(s):
        row = owned(s)
        length = lens[row]
        whole = r2[s].reshape(MSG, 128)
        fresh_k, fresh_v = whole[ROWS : ROWS + 128], whole[ROWS + 128 :]
        cachev[s, :, :128] = fresh_k
        cachev[s, :, 128:] = fresh_v
        cache_copy(s).start()
        nt = (((1,), (1,)), ((), ()))

        def page(j):
            return pool[pages[j, row]]

        position = lax.broadcasted_iota(jnp.int32, (1, 256), 1)
        t_key = lax.broadcasted_iota(jnp.int32, (BLOCK, 128), 1)
        t = lax.rem(lax.broadcasted_iota(jnp.int32, (BLOCK, 128), 0), SPAN_LEN)
        factor = SCALE * LOG2E
        for first in range(0, ROWS, BLOCK):
            q = whole[first : first + BLOCK]
            sc = lax.dot_general(q, fresh_k, nt, preferred_element_type=F32)
            sc = jnp.where(t_key <= t, sc, -jnp.inf)
            scores[:, PAGES * 128 :] = sc
            top = sc
            for j in range(0, PAGES, 2):
                keys = jnp.concatenate([page(j)[:, :128], page(j + 1)[:, :128]], axis=0)
                bias = jnp.where(position + j * 128 < length, 0.0, -jnp.inf)
                sc = lax.dot_general(q, keys, nt, preferred_element_type=F32) + bias
                scores[:, j * 128 : (j + 2) * 128] = sc
                top = jnp.maximum(top, jnp.maximum(sc[:, :128], sc[:, 128:]))
            highest = jnp.max(top, axis=1, keepdims=True) * factor
            w = jnp.exp2(scores[:, PAGES * 128 :] * factor - highest)
            total = w
            summed = jnp.dot(w.astype(BF), fresh_v, preferred_element_type=F32)
            for j in range(0, PAGES, 2):
                values = jnp.concatenate([page(j)[:, 128:], page(j + 1)[:, 128:]], axis=0)
                w = jnp.exp2(scores[:, j * 128 : (j + 2) * 128] * factor - highest)
                total = total + (w[:, :128] + w[:, 128:])
                summed = summed + jnp.dot(w.astype(BF), values, preferred_element_type=F32)
            total = jnp.sum(total, axis=1, keepdims=True)
            done = (summed / total).astype(BF).reshape(BLOCK // BACK, BACK, 128)
            om[s, first // BACK : (first + BLOCK) // BACK] = done
            result_out(s, first // BACK)

    def between(s, low, high):
        return pl.when((s >= low) & (s < high))

    def late_and_early(late, early, run):
        def one(n, carry):
            s = jnp.where(n == 0, late, early)

            @between(s, jnp.where(n == 0, EARLY, 0), jnp.where(n == 0, STEPS, EARLY))
            def _():
                run(s)

            return carry

        lax.fori_loop(0, 2, one, 0)

    def back_on(s):
        arrived(x_recv.at[2, s], r3)
        work3[...] = r3[s]
        for r in range(REPS):
            st4[s, r] = work3[owner[r * STEPS + s]]
        exchange(3, s, lambda r: st4.at[s, r], place(s))
        own_copy(s).start()

    def settle(s):
        for kind in range(8):
            y_copy(kind, s).wait_send()
        cache_copy(s).wait()
        arrived(x_send.at[2, s], om)

        @pl.when(s < EARLY)
        def _():
            arrived(x_send.at[0, s], msg)
            arrived(x_send.at[1, s], st2)

        @pl.when(s >= EARLY)
        def _():
            arrived(x_send.at[4, s], rh)
            arrived(x_send.at[5, s], sth)

    def finish(s):
        own_copy(s).wait()
        arrived(x_send.at[3, s], st4)
        arrived(x_recv.at[3, s], st4)

    def work(s):
        @pl.when(s < EARLY)
        def _():
            arrived(x_recv.at[1, s], r1)

        attend(s)
        r3[s, me] = om[s, me]

    def far_on(s):
        y_copy(3, s).wait_recv()
        y_copy(4, s).wait_recv()
        y_copy(7, s).start()

    def follow(it, carry):
        late_and_early(it - 2, it - 4, back_on)

        @between(it - 2, 0, EARLY)
        def _():
            s = it - 2
            arrived(x_recv.at[0, s], r1)
            work1[...] = r1[s]
            of = sources(s)
            for o in range(REPS):
                st2[s, o] = work1[of(o)]
            exchange(1, s, lambda o: st2.at[s, o], r2.at[s, me])
            r2[s, me] = st2[s, me]

        late_and_early(it - 2, it - 5, settle)
        late_and_early(it - 4, it - 7, finish)
        return carry

    def step(it, carry):
        @between(it, 0, STEPS)
        def _():
            y_copy(0, it).wait_recv()
            y_copy(3, it).start()
            y_copy(5, it).start()
            y_copy(1, it).wait_recv()
            y_copy(4, it).start()
            y_copy(6, it).start()

        @between(it - 1, 0, STEPS - 1)
        def _():
            far_on(it - 1)

        @between(it + 3, EARLY, STEPS)
        def _():
            hidden_on(it + 3)

        @between(it + 5, EARLY + 2, STEPS)
        def _():
            hidden_out(it + 5)

        @between(it, 0, STEPS)
        def _():
            for kind in (2, 5, 6):
                y_copy(kind, it).wait_recv()
            project_near(it)

        @between(it + 2, 2, STEPS)
        def _():
            @pl.when(it + 2 >= EARLY)
            def _():
                arrived(x_recv.at[5, it + 2], rh)

            near_send(it + 2)

        @between(it - 1, 0, STEPS)
        def _():
            s = it - 1
            y_copy(7, s).wait_recv()
            whole = project_far(s)

            @pl.when(s < EARLY)
            def _():
                msg[s] = whole
                exchange(0, s, lambda j: msg.at[s, j], r1.at[s, me])
                r1[s, me] = msg[s, me]

            @pl.when(s >= EARLY)
            def _():
                r2[s] = whole

        @pl.when(it == STEPS - 1)
        def _():
            far_on(it)

        late_and_early(it - 1, it - 3, work)
        last = STEPS - 1
        lax.fori_loop(
            jnp.where(it == last + 1, last, it), jnp.where(it == last, it, it + 1), follow, 0
        )
        return carry

    lax.fori_loop(0, STEPS + 4, step, 0)


def hand_over(back, fresh, out, cache, out_held, cache_held, sem):
    parts = []
    for s in range(0, STEPS, 2):
        rows = pl.ds(s * SPAN_LEN, 2 * SPAN_LEN)
        parts.append((back.at[rows], out_held.at[rows], out.at[rows]))
    for s in range(0, STEPS, 4):
        spans = pl.ds(s, 4)
        parts.append((fresh.at[spans], cache_held.at[spans], cache.at[spans]))
    first = [pltpu.make_async_copy(p[0], p[1], sem.at[0, i]) for i, p in enumerate(parts)]
    second = [pltpu.make_async_copy(p[1], p[2], sem.at[1, i]) for i, p in enumerate(parts)]
    for copy in first:
        copy.start()
    for one, two in zip(first, second):
        one.wait()
        two.start()
    for copy in second:
        copy.wait()


def trig_tables():
    i = np.arange(64, dtype=np.float64)
    frequency = np.concatenate([ROPE_BASE ** (-2.0 * i / HEAD_DIM)] * 2)
    angle = np.arange(SPAN_LEN, dtype=np.float64)[:, None] * frequency[None, :]
    wide = np.broadcast_to(frequency[None, :], (SPAN_LEN, HEAD_DIM))
    return np.stack([np.cos(angle), np.sin(angle), wide]).astype(np.float32)


def body(hidden, w_query, w_keyval, kv_pool, prefix_len, owner, block_table):
    v = pltpu.VMEM
    dma = pltpu.SemaphoreType.DMA
    any_spec = pl.BlockSpec(memory_space=pl.ANY)
    vmem = pl.BlockSpec(memory_space=pltpu.VMEM)
    shapes = (
        jax.ShapeDtypeStruct((STEPS * SPAN_LEN, GROUP * 128), BF),
        jax.ShapeDtypeStruct((STEPS, SPAN_LEN, 256), BF),
    )
    results = pl.pallas_call(
        kernel,
        out_shape=shapes,
        in_specs=[pl.BlockSpec(memory_space=pltpu.SMEM)] * 3 + [any_spec] * 4 + [vmem],
        out_specs=(any_spec, any_spec),
        scratch_shapes=[
            v((STEPS, SPAN_LEN, 8 * CHUNK), BF),
            v((8 * CHUNK, GROUP * 128), BF),
            v((8 * CHUNK, 256), BF),
            v((128, 128, 256), BF),
            v((2, SPAN_LEN, GROUP * 128), F32),
            v((2, SPAN_LEN, 256), F32),
            v((LATE, 2, SPAN_LEN, HALF), BF),
            v((LATE, REPS, 16, HALF), BF),
            v((LATE, REPS, 16, HALF), BF),
            v((EARLY, REPS, PIECE, 128), BF),
            v((EARLY, REPS, PIECE, 128), BF),
            v((EARLY, REPS, PIECE, 128), BF),
            v((STEPS, REPS, PIECE, 128), BF),
            v((STEPS, REPS, BACK, 128), BF),
            v((STEPS, REPS, BACK, 128), BF),
            v((STEPS, REPS, BACK, 128), BF),
            v((BLOCK, KEYS), F32),
            v((REPS, 16, HALF), BF),
            v((REPS, PIECE, 128), BF),
            v((REPS, BACK, 128), BF),
            v((STEPS, SPAN_LEN, 256), BF),
            dma((EARLY + 2 * LATE + 17,)),
            dma((2, STEPS)),
            pltpu.SemaphoreType.REGULAR((3,)),
            dma((8, STEPS)),
            dma((8, STEPS)),
            dma((6, STEPS)),
            dma((6, STEPS)),
        ],
        compiler_params=pltpu.CompilerParams(
            collective_id=0, has_side_effects=True, vmem_limit_bytes=62 * 1024 * 1024
        ),
        cost_estimate=pl.CostEstimate(
            flops=18_000_000_000, bytes_accessed=24_000_000, transcendentals=9_000_000
        ),
    )(prefix_len, owner, block_table.T, hidden, w_query, w_keyval, kv_pool, jnp.asarray(trig_tables()))
    return pl.pallas_call(
        hand_over,
        out_shape=shapes,
        in_specs=[any_spec] * 2,
        out_specs=(any_spec, any_spec),
        scratch_shapes=[v(shapes[0].shape, BF), v(shapes[1].shape, BF), dma((2, STEPS))],
    )(*results)


def solution(mesh):
    placed = (P("rep", "tp"), P(None, "tp"), P(None, "tp"), P("rep", None, "tp"), P(), P(), P())
    return jax.shard_map(
        body,
        mesh=mesh,
        in_specs=placed,
        out_specs=(P("rep", "tp"), P("rep", None, "tp")),
        check_vma=False,
    )
```
